512 devices in a mesh: leaf: 128 (over z, y, core), rep: 4 (over x).
Axes of the slice: x: 4, y: 4, z: 16, core: 2. Of those that a mesh axis runs over, the one named last changes fastest.
Arguments:
- basis: float32 [7, 128, 65536], P(None, 'rep', 'leaf'), may hold values from -6 to 6
- near_blocks: float32 [1024, 4, 4096], P('leaf'), may hold values from -0.375 to 0.375
- near_cols: int32 [1024, 4], P('leaf'), may hold values from 0 to 7
- bead_order: int32 [128, 512], P('leaf'), may hold values from 0 to 511, each once within a row
Outputs:
- factors: float32 [7, 128, 16384], P(None, 'rep', 'leaf')
The draws below stay inside these ranges and needn't reach their ends.
Inputs may be any that keep to these rules, and one draw needn't show every extreme that they name: `near_cols`: block columns within the leaf; a block row may name a column twice. `bead_order`: each leaf's row is a permutation of its 512 rows.
All inputs are finite; a program needn't handle non-finite values.
Results may differ from the reference program's by a relative error of at most 0.00012.
Values sent between devices are 32-bit elements; how exact they have to be, the bound alone decides.
No kernel may reach another device: no remote copies, remote signals or barrier semaphores. Data moves between devices by JAX's collectives and lax.ppermute only.
A program may use at most 64 MiB of HBM per device.

```python
import math
import jax
import jax.numpy as jnp
from jax import lax

K = 128
BLK = 64
NPR = 4
R_LEAF = 512
LEAVES = 128
LEVELS = 7
NBR = 8
ROWS = 65536


def with_ends(values, key, smallest, top_value):
    longest = values.shape.index(max(values.shape))
    spots = []
    for shift in (0, 1):
        where = [jax.random.randint(jax.random.fold_in(key, axis), (), 0, length) for axis, length in enumerate(values.shape)]
        where[longest] = (where[longest] + shift) % values.shape[longest]
        spots.append(tuple(where))
    return values.at[spots[0]].set(smallest).at[spots[1]].set(top_value)


def block_scale(stream_key, dims, pieces, low, largest):
    def one(dim, blocks):
        draws = jax.random.uniform(jax.random.fold_in(jax.random.fold_in(stream_key, 6), dim), (blocks,), jnp.float32, low / len(pieces), largest / len(pieces))
        return jnp.repeat(jnp.exp(draws), dims[dim] // blocks).reshape((-1,) + (1,) * (len(dims) - dim - 1))

    loudness = one(*pieces[0])
    for cut in pieces[1:]:
        loudness = loudness * one(*cut)
    return loudness


def normal_values(own_key, shape, deviation, reach, cuts=(), kind=jnp.bfloat16):
    array = deviation * jax.random.normal(own_key, shape, jnp.float32)
    if cuts:
        array = array * block_scale(own_key, shape, cuts, -0.22, 0.18)
    return jnp.clip(array, -reach, reach).astype(kind)


def setup_inputs(seed: int = 0) -> dict:
    key_list = jax.random.split(jax.random.key(seed), 5)
    return {
        "basis": normal_values(key_list[0], (LEVELS, K, ROWS), 1.0, 6.0, ((1, 4), (2, 128)), jnp.float32),
        "near_blocks": normal_values(key_list[1], (LEAVES * NBR, NPR, BLK * BLK), (BLK * NPR) ** -0.5, 0.375, ((0, 128),), jnp.float32),
        "near_cols": with_ends(jax.random.randint(key_list[2], (LEAVES * NBR, NPR), 0, NBR), jax.random.fold_in(key_list[2], 1), 0, NBR - 1).astype(jnp.int32),
        "bead_order": jax.vmap(lambda own: jax.random.permutation(own, R_LEAF))(jax.random.split(key_list[3], LEAVES)).reshape((LEAVES, R_LEAF)).astype(jnp.int32),
    }


def near_field(ordered, tiles_flat, near_cols):
    levels, width, rows = ordered.shape
    block_rows, per_row = near_cols.shape
    blk = rows // block_rows
    blocked = ordered.reshape(levels, width, block_rows, blk)
    picked = jnp.take(blocked, near_cols.reshape(-1), axis=2).reshape(levels, width, block_rows, per_row, blk)
    tiles = tiles_flat.reshape(block_rows, per_row, blk, blk)
    image = jnp.einsum('qnij,lcqnj->lcqi', tiles, picked, precision=lax.Precision.HIGHEST)
    return image.reshape(levels, width, rows)

def merge_pair(lower, upper, q_lower, q_upper):
    width = lower.shape[0]
    panels = jnp.concatenate([lower, upper], axis=0)
    zeros = jnp.zeros((width, width), jnp.float32)
    blocks = jnp.concatenate([jnp.concatenate([q_lower, zeros], axis=1), jnp.concatenate([zeros, q_upper], axis=1)], axis=0)
    capacity = blocks + jnp.dot(panels, panels.T, precision=lax.Precision.HIGHEST) / width
    factor = jnp.linalg.cholesky(capacity)
    whitened = jax.scipy.linalg.solve_triangular(factor, panels, lower=True)
    merged = jnp.eye(width, dtype=jnp.float32) + jnp.dot(whitened.T, whitened, precision=lax.Precision.HIGHEST) / width
    return (whitened, merged)

def reference(basis, near_blocks, near_cols, bead_order):
    levels, width, total = basis.shape
    leaves = bead_order.shape[0]
    rows = total // leaves
    block_rows = near_cols.shape[0] // leaves
    per_leaf = basis.reshape(levels, width, leaves, rows).transpose(2, 0, 1, 3)
    tiles = near_blocks.reshape(leaves, block_rows, near_blocks.shape[1], near_blocks.shape[2])
    columns = near_cols.reshape(leaves, block_rows, near_cols.shape[1])
    inv_root = 1.0 / math.sqrt(rows)

    def one_leaf(items):
        leaf_basis, order, leaf_tiles, leaf_cols = items
        ordered = jnp.take(leaf_basis, order, axis=2)
        image = near_field(ordered, leaf_tiles, leaf_cols)
        return jnp.einsum('lan,lbn->lab', ordered, image, precision=lax.Precision.HIGHEST) * inv_root
    panels = lax.map(one_leaf, (per_leaf, bead_order, tiles, columns))
    capacity = jnp.broadcast_to(jnp.eye(width, dtype=jnp.float32), (leaves, width, width))
    factors = []
    for level in range(levels):
        span = 2 ** level
        groups = leaves // span
        grouped = panels[:, level].reshape(groups, span, width, width).sum(axis=1) * (1.0 / math.sqrt(span))
        whitened, capacity = jax.vmap(merge_pair)(grouped[0::2], grouped[1::2], capacity[0::2], capacity[1::2])
        halves = whitened.reshape(groups, width, width)
        spread = jnp.repeat(halves, span, axis=0)
        factors.append(spread.transpose(2, 0, 1).reshape(width, leaves * width))
    return jnp.stack(factors)
```

```python
import functools
import math

import jax
import jax.numpy as jnp
from jax import lax
from jax.experimental import pallas as pl
from jax.experimental.pallas import tpu as pltpu
from jax.sharding import PartitionSpec as P

F32 = jnp.float32
BF16 = jnp.bfloat16
PANEL = 32
VMEM_BYTES = 48 * 1024 * 1024


def parts(x):
    high = x.astype(BF16)
    return high, (x - high.astype(F32)).astype(BF16)


def contract(a, b, dims):
    return lax.dot_general(a, b, (dims, ((), ())), preferred_element_type=F32)


def product(a, b, dims=((1,), (0,))):
    return contract(a[0], b[0], dims) + (contract(a[0], b[1], dims) + contract(a[1], b[0], dims))


def identity(n):
    rows = lax.broadcasted_iota(jnp.int32, (n, n), 0)
    return (rows == lax.broadcasted_iota(jnp.int32, (n, n), 1)).astype(F32)


def dense_kernel(cols_ref, blocks_ref, order_ref, high_ref, low_ref, columns):
    block_rows, per_row = cols_ref.shape
    blk = blocks_ref.shape[1]
    rows = block_rows * blk
    columns[...] = jnp.zeros_like(columns)
    for q in range(block_rows):
        for n in range(per_row):
            where = (cols_ref[q, n], slice(q * blk, (q + 1) * blk))
            columns[where] = columns[where] + blocks_ref[q * per_row + n]
    tree = jnp.concatenate([columns[c] for c in range(block_rows)], axis=1)
    bead = lax.broadcasted_iota(jnp.int32, (rows, rows), 0)
    select = (bead == order_ref[...]).astype(F32).astype(BF16)
    for piece, out in zip(parts(tree), (high_ref, low_ref)):
        moved = contract(select, piece, ((1,), (0,))).astype(BF16)
        out[...] = contract(moved, select, ((1,), (1,))).astype(BF16)


def panel_kernel(basis_ref, high_ref, low_ref, out_ref, first_ref):
    reps, levels, narrow, rows = basis_ref.shape
    scale = 1.0 / math.sqrt(rows)
    width = reps * narrow
    for level in range(levels):
        basis = parts(basis_ref[:, level].reshape(width, rows))
        image = product(basis, (high_ref[...], low_ref[...]))
        panel = product(parts(image), basis, ((1,), (1,))) * scale
        if level == 0:
            first_ref[...] = panel
            pair = parts(panel)
            panel = product(pair, pair, ((0,), (0,))) * (1.0 / width)
        out_ref[level] = panel


def level_kernel(last, side_ref, own_ref, other_ref, panel_ref, q_ref, *outs):
    width = panel_ref.shape[0]
    eye = identity(width)
    own, other = own_ref[0], other_ref[0]
    total = own + other
    bound = 1.0 + 2.0 * jnp.max(jnp.sum(jnp.abs(total), axis=0))
    if last:
        matrices = [eye + other]
    else:
        matrices = [eye + 2.0 * total, eye + total, eye + other]
    pairs = [parts(matrix) for matrix in matrices]
    rho = (bound - 1.0) / (bound + 1.0)
    step = 2.0 / (bound + 1.0)
    scale = 2.0 / (2.0 - rho * rho)
    start = tuple(scale * step * (2.0 * eye - step * matrix) for matrix in matrices)

    def go_on(carry):
        return carry[0] > 1e-3

    def refine(carry):
        rho, inverses = carry
        scale = 2.0 / (2.0 - rho * rho)
        new = []
        for pair, inverse in zip(pairs, inverses):
            x = parts(inverse)
            image = parts(product(pair, x))
            new.append(scale * (2.0 * inverse - product(x, image)))
        return (rho * rho / (2.0 - rho * rho), tuple(new))

    _, inverses = lax.while_loop(go_on, refine, (rho * rho / (2.0 - rho * rho), start))
    final = []
    for pair, inverse in zip(pairs, inverses):
        x = parts(inverse)
        residual = parts(eye - product(pair, x))
        final.append(inverse + product(x, residual))
    panel = parts(panel_ref[...])
    if not last:
        c_ref, pg_ref, next_panel_ref, next_q_ref, next_ref = outs
        root_half = math.sqrt(0.5)
        next_panel = (own_ref[1] + other_ref[1]) * root_half
        next_panel_ref[...] = next_panel
        pair = parts(next_panel)
        half = parts(0.5 * (eye + final[0]))
        next_ref[0] = product(pair, parts(product(half, pair)), ((0,), (0,))) * (1.0 / width)
        next_q_ref[...] = 2.0 * eye - final[1]
        for upper in range(1, next_ref.shape[0]):
            next_ref[upper] = (own_ref[upper + 1] + other_ref[upper + 1]) * root_half
    else:
        c_ref, pg_ref = outs
    gain = parts(jnp.where(side_ref[0] == 1, final[-1], eye))
    pg = product(panel, gain)
    pg_ref[...] = pg
    c_ref[...] = q_ref[...] + product(parts(pg), panel, ((1,), (1,))) * (1.0 / width)


def whiten_kernel(rep_ref, *refs):
    levels = (len(refs) - 2) // 2
    c_refs, x_refs, out_ref, turned = refs[:levels], refs[levels:2 * levels], refs[-2], refs[-1]
    width = c_refs[0].shape[0]
    narrow = out_ref.shape[1]
    lane = lax.broadcasted_iota(jnp.int32, (8, width), 1)
    sub = lax.broadcasted_iota(jnp.int32, (8, width), 0)
    count = PANEL // 8
    state = [jnp.concatenate([c[...], x[...]], axis=1) for c, x in zip(c_refs, x_refs)]
    done = [[] for _ in range(levels)]
    for top in range(0, width, PANEL):
        left = [[s[8 * j:8 * j + 8, :width] for j in range(count)] for s in state]
        right = [[s[8 * j:8 * j + 8, width:] for j in range(count)] for s in state]
        for kk in range(PANEL):
            k, block, row = top + kk, kk // 8, kk % 8
            for m in range(levels):
                v, w = left[m], right[m]
                line = jnp.broadcast_to(v[block][row:row + 1], (8, width))
                line_x = jnp.broadcast_to(w[block][row:row + 1], (8, width))
                pivot = jnp.broadcast_to(line[:, k:k + 1], (8, width))
                inverse = 1.0 / pivot
                for j in range(block, count):
                    if j == block and row == 7:
                        continue
                    factor = jnp.broadcast_to(v[j][:, k:k + 1], (8, width)) * inverse
                    if j == block:
                        factor = jnp.where(sub > row, factor, 0.0)
                    v[j] = v[j] - factor * line
                    w[j] = w[j] - factor * line_x
        for m in range(levels):
            for j in range(count):
                diagonal = jnp.sum(jnp.where(lane == sub + (top + 8 * j), left[m][j], 0.0), axis=1, keepdims=True)
                root = lax.rsqrt(diagonal)
                left[m][j] = left[m][j] * root
                right[m][j] = right[m][j] * root
            done[m].extend(right[m])
            rest = width - top - PANEL
            if rest:
                upper = jnp.concatenate(left[m], axis=0)
                both = jnp.concatenate([upper, jnp.concatenate(right[m], axis=0)], axis=1)
                change = product(parts(upper.T[top + PANEL:]), parts(both))
                state[m] = state[m][PANEL:] - change
    for m in range(levels):
        turned[m] = jnp.concatenate(done[m], axis=0).T
        out_ref[m] = turned[m, pl.ds(pl.multiple_of(rep_ref[0] * narrow, narrow), narrow), :]


def call(kernel, out_shape, n_smem, n_vmem, scratch=()):
    return pl.pallas_call(
        kernel,
        out_shape=out_shape,
        in_specs=[pl.BlockSpec(memory_space=pltpu.SMEM)] * n_smem
        + [pl.BlockSpec(memory_space=pltpu.VMEM)] * n_vmem,
        out_specs=jax.tree.map(lambda _: pl.BlockSpec(memory_space=pltpu.VMEM), out_shape),
        scratch_shapes=list(scratch),
        compiler_params=pltpu.CompilerParams(vmem_limit_bytes=VMEM_BYTES),
    )


def partner(leaf, bit):
    if bit == 0:
        return leaf ^ 1
    if bit == 1:
        return leaf ^ 2
    if bit == 2:
        return leaf ^ 6
    if bit == 4:
        return leaf ^ 24
    if bit == 6:
        z = leaf >> 3
        z = (z + 4) % 16 if z & 4 else (z - 4) % 16
        return z * 8 + (leaf & 7)
    return leaf ^ (1 << bit)


def swapped(value, axis, bit):
    pairs = [(source, partner(source, bit)) for source in range(lax.axis_size(axis))]
    return lax.ppermute(value, axis, pairs)


def local(basis, near_blocks, near_cols, bead_order):
    levels, narrow, rows = basis.shape
    block_rows, per_row = near_cols.shape
    blk = rows // block_rows
    gathered = lax.all_gather(basis, "rep", axis=0)
    width = gathered.shape[0] * narrow
    square = jax.ShapeDtypeStruct((width, width), F32)
    tiles = near_blocks.reshape(block_rows * per_row, blk, blk)
    dense = [jax.ShapeDtypeStruct((rows, rows), BF16)] * 2
    high, low = call(dense_kernel, dense, 1, 2, [pltpu.VMEM((block_rows, rows, blk), F32)])(
        near_cols, tiles, bead_order
    )
    sent, panel = call(
        panel_kernel, [jax.ShapeDtypeStruct((levels, width, width), F32), square], 0, 3
    )(gathered, high, low)
    leaf_index = lax.axis_index("leaf")
    rep_index = lax.axis_index("rep")
    q = jnp.eye(width, dtype=F32)
    c_list, x_list = [], []
    for bit in range(levels):
        last = bit == levels - 1
        received = swapped(sent, "leaf", bit)
        side = (leaf_index >> bit & 1).astype(jnp.int32).reshape(1)
        shapes = [square, square]
        if not last:
            shapes += [square, square, jax.ShapeDtypeStruct((levels - bit - 1, width, width), F32)]
        outs = call(functools.partial(level_kernel, last), shapes, 1, 4)(side, sent, received, panel, q)
        c_list.append(outs[0])
        x_list.append(outs[1])
        if not last:
            panel, q, sent = outs[2:]
    out = jax.ShapeDtypeStruct((levels, narrow, width), F32)
    return call(whiten_kernel, out, 1, 2 * levels, [pltpu.VMEM((levels, width, width), F32)])(
        rep_index.astype(jnp.int32).reshape(1), *c_list, *x_list
    )


def solution(mesh):
    return jax.shard_map(
        local,
        mesh=mesh,
        in_specs=(P(None, "rep", "leaf"), P("leaf", None, None), P("leaf", None), P("leaf", None)),
        out_specs=P(None, "rep", "leaf"),
        check_vma=False,
    )
```

```python
import functools
import math

import jax
import jax.numpy as jnp
from jax import lax
from jax.experimental import pallas as pl
from jax.experimental.pallas import tpu as pltpu
from jax.sharding import PartitionSpec as P

F32 = jnp.float32
BF16 = jnp.bfloat16
PANEL = 32
VMEM_BYTES = 48 * 1024 * 1024


def parts(x):
    high = x.astype(BF16)
    return high, (x - high.astype(F32)).astype(BF16)


def contract(a, b, dims):
    return lax.dot_general(a, b, (dims, ((), ())), preferred_element_type=F32)


def product(a, b, dims=((1,), (0,))):
    return contract(a[0], b[0], dims) + (contract(a[0], b[1], dims) + contract(a[1], b[0], dims))


def identity(n):
    rows = lax.broadcasted_iota(jnp.int32, (n, n), 0)
    return (rows == lax.broadcasted_iota(jnp.int32, (n, n), 1)).astype(F32)


def dense_kernel(cols_ref, blocks_ref, order_ref, high_ref, low_ref, columns):
    block_rows, per_row = cols_ref.shape
    blk = blocks_ref.shape[1]
    rows = block_rows * blk
    columns[...] = jnp.zeros_like(columns)
    for q in range(block_rows):
        for n in range(per_row):
            where = (cols_ref[q, n], slice(q * blk, (q + 1) * blk))
            columns[where] = columns[where] + blocks_ref[q * per_row + n]
    tree = jnp.concatenate([columns[c] for c in range(block_rows)], axis=1)
    bead = lax.broadcasted_iota(jnp.int32, (rows, rows), 0)
    select = (bead == order_ref[...]).astype(F32).astype(BF16)
    for piece, out in zip(parts(tree), (high_ref, low_ref)):
        moved = contract(select, piece, ((1,), (0,))).astype(BF16)
        out[...] = contract(moved, select, ((1,), (1,))).astype(BF16)


def panel_kernel(rep_ref, own_ref, *refs):
    reps = len(refs) - 3
    pieces, (high_ref, low_ref, out_ref, basis_scr) = (own_ref, *refs[: reps - 1]), refs[reps - 1:]
    own_levels, narrow, rows = own_ref.shape
    scale = 1.0 / math.sqrt(rows)
    width = reps * narrow
    rep = rep_ref[0]
    for shift, piece in enumerate(pieces):
        source = lax.rem(rep + reps - shift, reps)
        basis_scr[:, pl.ds(pl.multiple_of(source * narrow, narrow), narrow), :] = piece[...]
    panels = []
    for level in range(own_levels):
        basis = parts(basis_scr[level])
        image = product(basis, (high_ref[...], low_ref[...]))
        panels.append(product(parts(image), basis, ((1,), (1,))) * scale)
    pair = parts(panels[0])
    first = product(pair, pair, ((0,), (0,))) * (1.0 / width)
    out_ref[0] = panels[0]
    out_ref[1] = jnp.where(rep == 0, first, panels[1])


def level_kernel(first, last, side_ref, own_ref, pair_ref, *refs):
    width = own_ref.shape[1]
    eye = identity(width)
    side = side_ref[0]
    skip = 1 if first else 0
    if first:
        panel, q, outs = own_ref[0], eye, refs
    else:
        panel, q, outs = refs[0][...], refs[1][...], refs[2:]

    def theirs(n):
        return pair_ref[1 - side, n]

    def ours(n):
        return own_ref[n + skip]

    own, other = ours(0), theirs(0)
    total = own + other
    bound = 1.0 + 2.0 * jnp.max(jnp.sum(jnp.abs(total), axis=0))
    if last:
        matrices = [eye + other]
    else:
        matrices = [eye + 2.0 * total, eye + total, eye + other]
    pairs = [parts(matrix) for matrix in matrices]
    rho = (bound - 1.0) / (bound + 1.0)
    step = 2.0 / (bound + 1.0)
    scale = 2.0 / (2.0 - rho * rho)
    start = tuple(scale * step * (2.0 * eye - step * matrix) for matrix in matrices)

    def go_on(carry):
        return carry[0] > 1e-3

    def refine(carry):
        rho, inverses = carry
        scale = 2.0 / (2.0 - rho * rho)
        new = []
        for pair, inverse in zip(pairs, inverses):
            x = parts(inverse)
            image = parts(product(pair, x))
            new.append(scale * (2.0 * inverse - product(x, image)))
        return (rho * rho / (2.0 - rho * rho), tuple(new))

    _, inverses = lax.while_loop(go_on, refine, (rho * rho / (2.0 - rho * rho), start))
    final = []
    for pair, inverse in zip(pairs, inverses):
        x = parts(inverse)
        residual = parts(eye - product(pair, x))
        final.append(inverse + product(x, residual))
    panel = parts(panel)
    if not last:
        c_ref, pg_ref, next_panel_ref, next_q_ref, next_ref = outs
        root_half = math.sqrt(0.5)
        next_panel = (ours(1) + theirs(1)) * root_half
        next_panel_ref[...] = next_panel
        pair = parts(next_panel)
        half = parts(0.5 * (eye + final[0]))
        next_ref[0] = product(pair, parts(product(half, pair)), ((0,), (0,))) * (1.0 / width)
        next_q_ref[...] = 2.0 * eye - final[1]
        for upper in range(1, next_ref.shape[0]):
            next_ref[upper] = (ours(upper + 1) + theirs(upper + 1)) * root_half
    else:
        c_ref, pg_ref = outs
    gain = parts(jnp.where(side == 1, final[-1], eye))
    pg = product(panel, gain)
    pg_ref[...] = pg
    c_ref[...] = q + product(parts(pg), panel, ((1,), (1,))) * (1.0 / width)


def spread(x):
    return jnp.broadcast_to(x, (8, 128))


def reciprocal(x):
    guess = pl.reciprocal(x, approx=True)
    return guess * (2.0 - x * guess)


def whiten_kernel(rep_ref, *refs):
    levels = (len(refs) - 2) // 2
    c_refs, x_refs, out_ref, turned = refs[:levels], refs[levels:2 * levels], refs[-2], refs[-1]
    width = c_refs[0].shape[0]
    narrow = out_ref.shape[1]
    lane = lax.broadcasted_iota(jnp.int32, (8, width), 1)
    sub = lax.broadcasted_iota(jnp.int32, (8, width), 0)
    count = PANEL // 8
    state = [jnp.concatenate([c[...], x[...]], axis=1) for c, x in zip(c_refs, x_refs)]
    done = [[] for _ in range(levels)]
    for top in range(0, width, PANEL):
        left = [[s[8 * j:8 * j + 8, :width] for j in range(count)] for s in state]
        right = [[s[8 * j:8 * j + 8, width:] for j in range(count)] for s in state]
        for kk in range(0, PANEL, 2):
            k, block, row = top + kk, kk // 8, kk % 8
            for m in range(levels):
                v, w = left[m], right[m]
                line0, line1 = spread(v[block][row:row + 1]), spread(v[block][row + 1:row + 2])
                line0_x, line1_x = spread(w[block][row:row + 1]), spread(w[block][row + 1:row + 2])
                p00, p01 = spread(line0[:, k:k + 1]), spread(line0[:, k + 1:k + 2])
                p11 = spread(line1[:, k + 1:k + 2])
                inverse = reciprocal(p00 * p11 - p01 * p01)
                i00, i01, i11 = p11 * inverse, p01 * inverse, p00 * inverse
                ratio = p01 * reciprocal(p00)
                for j in range(block, count):
                    if j == block and row == 6:
                        f0 = jnp.where(sub == row + 1, ratio, 0.0)
                        v[j] = v[j] - f0 * line0
                        w[j] = w[j] - f0 * line0_x
                        continue
                    c0, c1 = spread(v[j][:, k:k + 1]), spread(v[j][:, k + 1:k + 2])
                    f0, f1 = i00 * c0 - i01 * c1, i11 * c1 - i01 * c0
                    if j == block:
                        f0 = jnp.where(sub > row + 1, f0, jnp.where(sub == row + 1, ratio, 0.0))
                        f1 = jnp.where(sub > row + 1, f1, 0.0)
                    v[j] = v[j] - f0 * line0 - f1 * line1
                    w[j] = w[j] - f0 * line0_x - f1 * line1_x
        for m in range(levels):
            for j in range(count):
                diagonal = jnp.sum(jnp.where(lane == sub + (top + 8 * j), left[m][j], 0.0), axis=1, keepdims=True)
                root = lax.rsqrt(diagonal)
                left[m][j] = left[m][j] * root
                right[m][j] = right[m][j] * root
            done[m].extend(right[m])
            rest = width - top - PANEL
            if rest:
                upper = jnp.concatenate(left[m], axis=0)
                both = jnp.concatenate([upper, jnp.concatenate(right[m], axis=0)], axis=1)
                change = product(parts(upper.T[top + PANEL:]), parts(both))
                state[m] = state[m][PANEL:] - change
    for m in range(levels):
        turned[m] = jnp.concatenate(done[m], axis=0).T
        out_ref[m] = turned[m, pl.ds(pl.multiple_of(rep_ref[0] * narrow, narrow), narrow), :]


def call(kernel, out_shape, n_smem, n_vmem, scratch=()):
    return pl.pallas_call(
        kernel,
        out_shape=out_shape,
        in_specs=[pl.BlockSpec(memory_space=pltpu.SMEM)] * n_smem
        + [pl.BlockSpec(memory_space=pltpu.VMEM)] * n_vmem,
        out_specs=jax.tree.map(lambda _: pl.BlockSpec(memory_space=pltpu.VMEM), out_shape),
        scratch_shapes=list(scratch),
        compiler_params=pltpu.CompilerParams(vmem_limit_bytes=VMEM_BYTES),
    )


def partner(leaf, bit):
    if bit == 0:
        return leaf ^ 1
    if bit == 1:
        return leaf ^ 2
    if bit == 2:
        return leaf ^ 6
    if bit == 4:
        return leaf ^ 24
    if bit == 6:
        z = leaf >> 3
        z = (z + 4) % 16 if z & 4 else (z - 4) % 16
        return z * 8 + (leaf & 7)
    return leaf ^ (1 << bit)


def pair_gathered(value, axis, bit):
    leaves = range(lax.axis_size(axis))
    groups = [[leaf, partner(leaf, bit)] for leaf in leaves if not leaf >> bit & 1]
    return lax.all_gather(value, axis, axis=0, axis_index_groups=groups)


def local(basis, near_blocks, near_cols, bead_order):
    levels, narrow, rows = basis.shape
    block_rows, per_row = near_cols.shape
    blk = rows // block_rows
    reps = lax.axis_size("rep")
    width = reps * narrow
    leaf_index = lax.axis_index("leaf")
    rep_index = lax.axis_index("rep")
    rep_scalar = rep_index.astype(jnp.int32).reshape(1)
    square = jax.ShapeDtypeStruct((width, width), F32)

    def levels_of(rep):
        return lax.dynamic_slice_in_dim(basis, jnp.maximum(2 * rep - 1, 0), 2, 0)

    pieces = [levels_of(rep_index)]
    for shift in range(1, reps):
        pairs = [(source, (source + shift) % reps) for source in range(reps)]
        pieces.append(lax.ppermute(levels_of(lax.rem(rep_index + shift, reps)), "rep", pairs))
    tiles = near_blocks.reshape(block_rows * per_row, blk, blk)
    dense = [jax.ShapeDtypeStruct((rows, rows), BF16)] * 2
    high, low = call(dense_kernel, dense, 1, 2, [pltpu.VMEM((block_rows, rows, blk), F32)])(
        near_cols, tiles, bead_order
    )
    two = jax.ShapeDtypeStruct((2, width, width), F32)
    mine = call(panel_kernel, two, 1, reps + 2, [pltpu.VMEM((2, width, rows), F32)])(
        rep_scalar, *pieces, high, low
    )
    sent = lax.all_gather(mine, "rep", axis=0, tiled=True)
    state = []
    c_list, x_list = [], []
    for bit in range(levels):
        first, last = bit == 0, bit == levels - 1
        pair = pair_gathered(sent[1:] if first else sent, "leaf", bit)
        side = (leaf_index >> bit & 1).astype(jnp.int32).reshape(1)
        shapes = [square, square]
        if not last:
            shapes += [square, square, jax.ShapeDtypeStruct((levels - bit - 1, width, width), F32)]
        kernel = functools.partial(level_kernel, first, last)
        c, x, *rest = call(kernel, shapes, 1, 2 + len(state))(side, sent, pair, *state)
        c_list.append(c)
        x_list.append(x)
        if not last:
            *state, sent = rest
    out = jax.ShapeDtypeStruct((levels, narrow, width), F32)
    return call(whiten_kernel, out, 1, 2 * levels, [pltpu.VMEM((levels, width, width), F32)])(
        rep_scalar, *c_list, *x_list
    )


def solution(mesh):
    return jax.shard_map(
        local,
        mesh=mesh,
        in_specs=(P(None, "rep", "leaf"), P("leaf", None, None), P("leaf", None), P("leaf", None)),
        out_specs=P(None, "rep", "leaf"),
        check_vma=False,
    )
```

```python
import functools
import math

import jax
import jax.numpy as jnp
from jax import lax
from jax.experimental import pallas as pl
from jax.experimental.pallas import tpu as pltpu
from jax.sharding import PartitionSpec as P

F32 = jnp.float32
BF16 = jnp.bfloat16
PANEL = 32
EXCHANGE = ("pair",) * 7
VMEM_BYTES = 48 * 1024 * 1024


def parts(x):
    high = x.astype(BF16)
    return high, (x - high.astype(F32)).astype(BF16)


def contract(a, b, dims):
    return lax.dot_general(a, b, (dims, ((), ())), preferred_element_type=F32)


def product(a, b, dims=((1,), (0,))):
    return contract(a[0], b[0], dims) + (contract(a[0], b[1], dims) + contract(a[1], b[0], dims))


def identity(n):
    rows = lax.broadcasted_iota(jnp.int32, (n, n), 0)
    return (rows == lax.broadcasted_iota(jnp.int32, (n, n), 1)).astype(F32)


def dense_kernel(cols_ref, blocks_ref, order_ref, high_ref, low_ref, columns):
    block_rows, per_row = cols_ref.shape
    blk = blocks_ref.shape[1]
    rows = block_rows * blk
    columns[...] = jnp.zeros_like(columns)
    for q in range(block_rows):
        for n in range(per_row):
            where = (cols_ref[q, n], slice(q * blk, (q + 1) * blk))
            columns[where] = columns[where] + blocks_ref[q * per_row + n]
    tree = jnp.concatenate([columns[c] for c in range(block_rows)], axis=1)
    bead = lax.broadcasted_iota(jnp.int32, (rows, rows), 0)
    select = (bead == order_ref[...]).astype(F32).astype(BF16)
    for piece, out in zip(parts(tree), (high_ref, low_ref)):
        moved = contract(select, piece, ((1,), (0,))).astype(BF16)
        out[...] = contract(moved, select, ((1,), (1,))).astype(BF16)


def panel_kernel(rep_ref, own_ref, *refs):
    reps = len(refs) - 3
    pieces, (high_ref, low_ref, out_ref, basis_scr) = (own_ref, *refs[: reps - 1]), refs[reps - 1:]
    own_levels, narrow, rows = own_ref.shape
    scale = 1.0 / math.sqrt(rows)
    width = reps * narrow
    rep = rep_ref[0]
    for shift, piece in enumerate(pieces):
        source = lax.rem(rep + reps - shift, reps)
        basis_scr[:, pl.ds(pl.multiple_of(source * narrow, narrow), narrow), :] = piece[...]
    panels = []
    for level in range(own_levels):
        basis = parts(basis_scr[level])
        image = product(basis, (high_ref[...], low_ref[...]))
        panels.append(product(parts(image), basis, ((1,), (1,))) * scale)
    pair = parts(panels[0])
    first = product(pair, pair, ((0,), (0,))) * (1.0 / width)
    out_ref[0] = panels[0]
    out_ref[1] = jnp.where(rep == 0, first, panels[1])


def level_kernel(first, last, kind, split, side_ref, core_ref, own_ref, pair_ref, *refs):
    width = own_ref.shape[1]
    eye = identity(width)
    side = side_ref[0]
    skip = 1 if first else 0
    if first:
        panel, outs = own_ref[0], refs
    else:
        panel, outs = refs[0][...], refs[1:]

    def theirs(n):
        if kind == "other":
            return pair_ref[n]
        if kind == "pair":
            return pair_ref[1 - side, n]
        if kind == "halfother":
            return jnp.concatenate([pair_ref[core, n] for core in range(2)], axis=0)
        return jnp.concatenate([pair_ref[core, 1 - side, n] for core in range(2)], axis=0)

    def ours(n):
        return own_ref[n + skip]

    own, other = ours(0), theirs(0)
    total = own + other
    bound = 1.0 + 2.0 * jnp.max(jnp.sum(jnp.abs(total), axis=0))
    if last:
        matrices = [eye + other]
    else:
        matrices = [eye + other, eye + total, eye + 2.0 * total]
        root_half = math.sqrt(0.5)
        next_panel = (ours(1) + theirs(1)) * root_half
    step = 2.0 / (bound + 1.0)
    start = ((bound - 1.0) / (bound + 1.0), tuple((step * eye, eye - step * matrix) for matrix in matrices))

    def go_on(carry):
        return carry[0] > 1e-2

    def refine(carry):
        rho, inverses = carry
        scale = 2.0 / (2.0 - rho * rho)
        new = []
        for inverse, residual in inverses:
            e = parts(residual)
            better = scale * (inverse + product(parts(inverse), e))
            new.append((better, (1.0 - scale) * eye + scale * product(e, e)))
        return (rho * rho / (2.0 - rho * rho), tuple(new))

    _, inverses = lax.while_loop(go_on, refine, start)
    pairs = [parts(matrix) for matrix in matrices]

    def correct(_, found):
        new = []
        for inverse, pair in zip(found, pairs):
            x = parts(inverse)
            new.append(inverse + product(x, parts(eye - product(pair, x))))
        return tuple(new)

    extra = jnp.where(bound > 200.0, 3, 0)
    inverses = lax.fori_loop(0, extra, correct, tuple(inverse for inverse, _ in inverses))
    x = [parts(inverse) for inverse in inverses]
    residuals = [parts(eye - product(pair, inverse)) for pair, inverse in zip(pairs, x)]
    if not last:
        next_panel_ref, next_q_ref, next_ref = outs[1:4]
        p = parts(next_panel)
        r = residuals[2]
        y = product(x[2], p)
        ry, rp = product(r, parts(y)), product(r, p)
        sum_y = next_panel + y
        plain = product(p, parts(sum_y), ((0,), (0,)))
        bent = product(parts(ry), parts(next_panel + rp), ((0,), (0,)))
        next_ref[0] = (plain + bent) * (0.5 / width)
        next_panel_ref[...] = next_panel
        for upper in range(1, next_ref.shape[0]):
            next_ref[upper] = (ours(upper + 1) + theirs(upper + 1)) * root_half
        if split:
            half_rows = width // 2
            outs[4][...] = next_ref[:, pl.ds(pl.multiple_of(core_ref[0] * half_rows, half_rows), half_rows), :]
        r = residuals[1]
        both = eye - product(pairs[1], x[1]) + product(r, r)
        next_q_ref[...] = 2.0 * eye - (inverses[1] + product(x[1], parts(both)))
    r = residuals[0]
    v = product(parts(panel), x[0])
    vr = product(parts(v), r)
    gained = v + vr + product(parts(vr), r)
    outs[0][...] = jnp.where(side == 1, gained, panel)


def spread(x):
    return jnp.broadcast_to(x, (8, 128))


def reciprocal(x):
    guess = pl.reciprocal(x, approx=True)
    return guess * (2.0 - x * guess)


def eliminate(v, w, k, block, row, sub):
    count = len(v)
    line = [spread(v[block][row + i:row + i + 1]) for i in range(4)]
    line_w = [spread(w[block][row + i:row + i + 1]) for i in range(4)] if w else []
    column = {j: [spread(v[j][:, k + i:k + i + 1]) for i in range(4)] for j in range(block, count)}
    p = {(i, h): spread(column[block][i][row + h:row + h + 1]) for i in range(4) for h in range(i, 4)}
    inverse = reciprocal(p[0, 0] * p[1, 1] - p[0, 1] * p[0, 1])
    i00, i01, i11 = p[1, 1] * inverse, -(p[0, 1] * inverse), p[0, 0] * inverse
    f02, f12 = i00 * p[0, 2] + i01 * p[1, 2], i01 * p[0, 2] + i11 * p[1, 2]
    f03, f13 = i00 * p[0, 3] + i01 * p[1, 3], i01 * p[0, 3] + i11 * p[1, 3]
    s22 = p[2, 2] - (p[0, 2] * f02 + p[1, 2] * f12)
    s23 = p[2, 3] - (p[0, 2] * f03 + p[1, 2] * f13)
    s33 = p[3, 3] - (p[0, 3] * f03 + p[1, 3] * f13)
    inverse = reciprocal(s22 * s33 - s23 * s23)
    j22, j23, j33 = s33 * inverse, -(s23 * inverse), s22 * inverse
    f01, f23 = p[0, 1] * reciprocal(p[0, 0]), s23 * reciprocal(s22)
    for lines in (line, line_w)[:2 if w else 1]:
        lines[2] = lines[2] - f02 * lines[0] - f12 * lines[1]
        lines[3] = lines[3] - f03 * lines[0] - f13 * lines[1]
    for j in range(block, count):
        c = column[j]
        if j > block or row == 0:
            g0, g1 = i00 * c[0] + i01 * c[1], i01 * c[0] + i11 * c[1]
            e2 = c[2] - c[0] * f02 - c[1] * f12
            e3 = c[3] - c[0] * f03 - c[1] * f13
            g2, g3 = j22 * e2 + j23 * e3, j23 * e2 + j33 * e3
        else:
            g0 = g1 = g2 = g3 = 0.0
        if j == block:
            inside = jnp.where(sub == row + 1, f01, jnp.where(sub == row + 2, f02, jnp.where(sub == row + 3, f03, 0.0)))
            g0 = jnp.where(sub > row + 3, g0, inside)
            g1 = jnp.where(sub > row + 3, g1, jnp.where(sub == row + 2, f12, jnp.where(sub == row + 3, f13, 0.0)))
            g2 = jnp.where(sub > row + 3, g2, jnp.where(sub == row + 3, f23, 0.0))
            g3 = jnp.where(sub > row + 3, g3, 0.0)
        v[j] = v[j] - g0 * line[0] - g1 * line[1] - g2 * line[2] - g3 * line[3]
        if w:
            w[j] = w[j] - g0 * line_w[0] - g1 * line_w[1] - g2 * line_w[2] - g3 * line_w[3]


def whiten_kernel(levels, rep_ref, *refs):
    x_refs, p_refs, q_refs = refs[:levels], refs[levels:2 * levels], refs[2 * levels:-1]
    out_ref = refs[-1]
    width = x_refs[0].shape[0]
    narrow = out_ref.shape[1]
    lane = lax.broadcasted_iota(jnp.int32, (8, width), 1)
    sub = lax.broadcasted_iota(jnp.int32, (8, width), 0)
    count = PANEL // 8
    rows = lax.broadcasted_iota(jnp.int32, (width, width), 0)
    lanes = lax.broadcasted_iota(jnp.int32, (width, width), 1)
    select = ((rows == lanes + rep_ref[0] * narrow) & (lanes < narrow)).astype(F32).astype(BF16)
    state, columns = [], []
    for m in range(levels):
        x, p = x_refs[m][...], p_refs[m]
        p = p[0] if len(p.shape) == 3 else p[...]
        q = q_refs[m - 1][...] if m else identity(width)
        pair = parts(x)
        state.append(q + product(pair, parts(p), ((1,), (1,))) * (1.0 / width))
        rest = parts(x - pair[0].astype(F32) - pair[1].astype(F32))[0]
        columns.append(sum(contract(piece, select, ((1,), (0,))) for piece in (*pair, rest)))
    done = [[] for _ in range(levels)]
    for top in range(0, width, PANEL):
        left = [[s[8 * j:8 * j + 8] for j in range(count)] for s in state]
        right = [[c[8 * j:8 * j + 8] for j in range(count)] if top == 0 else [] for c in columns]
        for kk in range(0, PANEL, 4):
            for m in range(levels):
                eliminate(left[m], right[m], top + kk, kk // 8, kk % 8, sub)
        for m in range(levels):
            for j in range(count):
                diagonal = jnp.sum(jnp.where(lane == sub + (top + 8 * j), left[m][j], 0.0), axis=1, keepdims=True)
                root = lax.rsqrt(diagonal)
                left[m][j] = left[m][j] * root
                if top == 0:
                    right[m][j] = right[m][j] * root
            upper = jnp.concatenate(left[m], axis=0)
            both = upper
            if top == 0:
                both = jnp.where(lanes[:PANEL] < narrow, jnp.concatenate(right[m], axis=0), upper)
            done[m].append(both)
            if top + PANEL < width:
                rest = state[m][PANEL:]
                if top == 0:
                    rest = jnp.where(lanes[PANEL:] < narrow, columns[m][PANEL:], rest)
                state[m] = rest - product(parts(upper.T[top + PANEL:]), parts(both))
    for m in range(levels):
        out_ref[m] = jnp.concatenate(done[m], axis=0).T[:narrow]


def call(kernel, out_shape, n_smem, n_vmem, scratch=()):
    return pl.pallas_call(
        kernel,
        out_shape=out_shape,
        in_specs=[pl.BlockSpec(memory_space=pltpu.SMEM)] * n_smem
        + [pl.BlockSpec(memory_space=pltpu.VMEM)] * n_vmem,
        out_specs=jax.tree.map(lambda _: pl.BlockSpec(memory_space=pltpu.VMEM), out_shape),
        scratch_shapes=list(scratch),
        compiler_params=pltpu.CompilerParams(vmem_limit_bytes=VMEM_BYTES),
    )


def partner(leaf, bit):
    if bit == 0:
        return leaf ^ 1
    if bit == 1:
        return leaf ^ 2
    if bit == 2:
        return leaf ^ 6
    if bit == 4:
        return leaf ^ 24
    if bit == 6:
        z = leaf >> 3
        z = (z + 4) % 16 if z & 4 else (z - 4) % 16
        return z * 8 + (leaf & 7)
    return leaf ^ (1 << bit)


def pair_gathered(value, axis, bit):
    leaves = range(lax.axis_size(axis))
    groups = [[leaf, partner(leaf, bit)] for leaf in leaves if not leaf >> bit & 1]
    return lax.all_gather(value, axis, axis=0, axis_index_groups=groups)


def swapped(value, axis, bit):
    pairs = [(source, partner(source, bit)) for source in range(lax.axis_size(axis))]
    return lax.ppermute(value, axis, pairs)


def local(basis, near_blocks, near_cols, bead_order):
    levels, narrow, rows = basis.shape
    block_rows, per_row = near_cols.shape
    blk = rows // block_rows
    reps = lax.axis_size("rep")
    width = reps * narrow
    leaf_index = lax.axis_index("leaf")
    rep_index = lax.axis_index("rep")
    rep_scalar = rep_index.astype(jnp.int32).reshape(1)
    square = jax.ShapeDtypeStruct((width, width), F32)

    def levels_of(rep):
        return lax.dynamic_slice_in_dim(basis, jnp.maximum(2 * rep - 1, 0), 2, 0)

    pieces = [levels_of(rep_index)]
    for shift in range(1, reps):
        pairs = [(source, (source + shift) % reps) for source in range(reps)]
        pieces.append(lax.ppermute(levels_of(lax.rem(rep_index + shift, reps)), "rep", pairs))
    tiles = near_blocks.reshape(block_rows * per_row, blk, blk)
    dense = [jax.ShapeDtypeStruct((rows, rows), BF16)] * 2
    high, low = call(dense_kernel, dense, 1, 2, [pltpu.VMEM((block_rows, rows, blk), F32)])(
        near_cols, tiles, bead_order
    )
    two = jax.ShapeDtypeStruct((2, width, width), F32)
    mine = call(panel_kernel, two, 1, reps + 2, [pltpu.VMEM((2, width, rows), F32)])(
        rep_scalar, *pieces, high, low
    )
    sent = lax.all_gather(mine, "rep", axis=0, tiled=True)
    core = (leaf_index & 1).astype(jnp.int32).reshape(1)
    half = panel = None
    x_list, p_list, q_list = [], [sent], []
    for bit in range(levels):
        first, last = bit == 0, bit == levels - 1
        kind = EXCHANGE[bit]
        value = half if kind.startswith("half") else sent[1:] if first else sent
        pair = (swapped if kind.endswith("other") else pair_gathered)(value, "leaf", bit)
        if kind.startswith("half"):
            pair = pair_gathered(pair, "leaf", 0)
        side = (leaf_index >> bit & 1).astype(jnp.int32).reshape(1)
        split = not last and EXCHANGE[bit + 1].startswith("half")
        shapes = [square]
        if not last:
            count = levels - bit - 1
            shapes += [square, square, jax.ShapeDtypeStruct((count, width, width), F32)]
            if split:
                shapes.append(jax.ShapeDtypeStruct((count, width // 2, width), F32))
        kernel = functools.partial(level_kernel, first, last, kind, split)
        state = [] if first else [panel]
        x, *rest = call(kernel, shapes, 2, 2 + len(state))(side, core, sent, pair, *state)
        x_list.append(x)
        if not last:
            panel, q, sent = rest[:3]
            half = rest[-1]
            p_list.append(panel)
            q_list.append(q)
    out = jax.ShapeDtypeStruct((levels, narrow, width), F32)
    return call(functools.partial(whiten_kernel, levels), out, 1, 3 * levels - 1)(
        rep_scalar, *x_list, *p_list, *q_list
    )


def solution(mesh):
    return jax.shard_map(
        local,
        mesh=mesh,
        in_specs=(P(None, "rep", "leaf"), P("leaf", None, None), P("leaf", None), P("leaf", None)),
        out_specs=P(None, "rep", "leaf"),
        check_vma=False,
    )
```

```python
import functools
import math

import jax
import jax.numpy as jnp
from jax import lax
from jax.experimental import pallas as pl
from jax.experimental.pallas import tpu as pltpu
from jax.sharding import PartitionSpec as P

F32 = jnp.float32
BF16 = jnp.bfloat16
PANEL = 32
EXCHANGE = ("pair",) * 7
VMEM_BYTES = 48 * 1024 * 1024


def parts(x):
    high = x.astype(BF16)
    return high, (x - high.astype(F32)).astype(BF16)


def contract(a, b, dims):
    return lax.dot_general(a, b, (dims, ((), ())), preferred_element_type=F32)


def product(a, b, dims=((1,), (0,))):
    return contract(a[0], b[0], dims) + (contract(a[0], b[1], dims) + contract(a[1], b[0], dims))


def wide_product(a, b, dims=((1,), (0,))):
    (ca,), (cb,) = dims
    above = jnp.concatenate([b[0], b[1]], axis=1 - cb)
    below = jnp.concatenate([b[0], jnp.zeros_like(b[1])], axis=1 - cb)
    both = contract(jnp.concatenate([a[0], a[1]], axis=ca), jnp.concatenate([above, below], axis=cb), dims)
    half = both.shape[1] // 2
    return both[:, :half] + both[:, half:]


def identity(n):
    rows = lax.broadcasted_iota(jnp.int32, (n, n), 0)
    return (rows == lax.broadcasted_iota(jnp.int32, (n, n), 1)).astype(F32)


def dense_kernel(cols_ref, blocks_ref, order_ref, high_ref, low_ref, columns):
    block_rows, per_row = cols_ref.shape
    blk = blocks_ref.shape[1]
    rows = block_rows * blk
    columns[...] = jnp.zeros_like(columns)
    for q in range(block_rows):
        for n in range(per_row):
            where = (cols_ref[q, n], slice(q * blk, (q + 1) * blk))
            columns[where] = columns[where] + blocks_ref[q * per_row + n]
    tree = jnp.concatenate([columns[c] for c in range(block_rows)], axis=1)
    bead = lax.broadcasted_iota(jnp.int32, (rows, rows), 0)
    select = (bead == order_ref[...]).astype(F32).astype(BF16)
    for piece, out in zip(parts(tree), (high_ref, low_ref)):
        moved = contract(select, piece, ((1,), (0,))).astype(BF16)
        out[...] = contract(moved, select, ((1,), (1,))).astype(BF16)


def panel_kernel(rep_ref, own_ref, *refs):
    reps = len(refs) - 3
    pieces, (high_ref, low_ref, out_ref, basis_scr) = (own_ref, *refs[: reps - 1]), refs[reps - 1:]
    own_levels, narrow, rows = own_ref.shape
    scale = 1.0 / math.sqrt(rows)
    width = reps * narrow
    rep = rep_ref[0]
    for shift, piece in enumerate(pieces):
        source = lax.rem(rep + reps - shift, reps)
        basis_scr[:, pl.ds(pl.multiple_of(source * narrow, narrow), narrow), :] = piece[...]
    panels = []
    for level in range(own_levels):
        basis = parts(basis_scr[level])
        image = product(basis, (high_ref[...], low_ref[...]))
        panels.append(product(parts(image), basis, ((1,), (1,))) * scale)
    pair = parts(panels[0])
    first = product(pair, pair, ((0,), (0,))) * (1.0 / width)
    out_ref[0] = panels[0]
    out_ref[1] = jnp.where(rep == 0, first, panels[1])


def level_kernel(first, last, kind, split, side_ref, core_ref, own_ref, pair_ref, *refs):
    width = own_ref.shape[1]
    eye = identity(width)
    side = side_ref[0]
    skip = 1 if first else 0
    if first:
        panel, outs = own_ref[0], refs
    else:
        panel, outs = refs[0][...], refs[1:]

    def theirs(n):
        if kind == "other":
            return pair_ref[n]
        if kind == "pair":
            return pair_ref[1 - side, n]
        if kind == "halfother":
            return jnp.concatenate([pair_ref[core, n] for core in range(2)], axis=0)
        return jnp.concatenate([pair_ref[core, 1 - side, n] for core in range(2)], axis=0)

    def ours(n):
        return own_ref[n + skip]

    own, other = ours(0), theirs(0)
    total = own + other
    bound = 1.0 + 2.0 * jnp.max(jnp.sum(jnp.abs(total), axis=0))
    if last:
        matrices = [eye + other]
    else:
        matrices = [eye + other, eye + total, eye + 2.0 * total]
        root_half = math.sqrt(0.5)
        next_panel = (ours(1) + theirs(1)) * root_half
    step = 2.0 / (bound + 1.0)
    rho = 1.0 - step
    scale = 2.0 / (2.0 - rho * rho)
    begun = []
    for matrix in matrices:
        residual = eye - step * matrix
        e = parts(residual)
        begun.append(((scale * step) * (eye + residual), (1.0 - scale) * eye + scale * wide_product(e, e)))
    start = (0.5 * scale * rho * rho, tuple(begun))

    def go_on(carry):
        return carry[0] > 1e-2

    def refine(carry):
        rho, inverses = carry
        scale = 2.0 / (2.0 - rho * rho)
        new = []
        for inverse, residual in inverses:
            e = parts(residual)
            better = scale * (inverse + wide_product(parts(inverse), e))
            new.append((better, (1.0 - scale) * eye + scale * wide_product(e, e)))
        return (0.5 * scale * rho * rho, tuple(new))

    _, inverses = lax.while_loop(go_on, refine, start)
    pairs = [parts(matrix) for matrix in matrices]

    def correct(_, found):
        new = []
        for inverse, pair in zip(found, pairs):
            x = parts(inverse)
            new.append(inverse + wide_product(x, parts(eye - wide_product(pair, x))))
        return tuple(new)

    extra = jnp.where(bound > 200.0, 3, 0)
    inverses = lax.fori_loop(0, extra, correct, tuple(inverse for inverse, _ in inverses))
    x = [parts(inverse) for inverse in inverses]
    residuals = [parts(eye - wide_product(pair, inverse)) for pair, inverse in zip(pairs, x)]
    if not last:
        next_panel_ref, next_q_ref, next_ref = outs[1:4]
        p = parts(next_panel)
        r = residuals[2]
        y = wide_product(x[2], p)
        ry, rp = wide_product(r, parts(y)), wide_product(r, p)
        sum_y = next_panel + y
        plain = wide_product(p, parts(sum_y), ((0,), (0,)))
        bent = wide_product(parts(ry), parts(next_panel + rp), ((0,), (0,)))
        next_ref[0] = (plain + bent) * (0.5 / width)
        next_panel_ref[...] = next_panel
        for upper in range(1, next_ref.shape[0]):
            next_ref[upper] = (ours(upper + 1) + theirs(upper + 1)) * root_half
        if split:
            half_rows = width // 2
            outs[4][...] = next_ref[:, pl.ds(pl.multiple_of(core_ref[0] * half_rows, half_rows), half_rows), :]
        r = residuals[1]
        both = eye - wide_product(pairs[1], x[1]) + wide_product(r, r)
        next_q_ref[...] = 2.0 * eye - (inverses[1] + wide_product(x[1], parts(both)))
    r = residuals[0]
    v = wide_product(parts(panel), x[0])
    vr = wide_product(parts(v), r)
    gained = v + vr + wide_product(parts(vr), r)
    outs[0][...] = jnp.where(side == 1, gained, panel)


def spread(x):
    return jnp.broadcast_to(x, (8, 128))


def reciprocal(x):
    guess = pl.reciprocal(x, approx=True)
    return guess * (2.0 - x * guess)


def eliminate(v, w, k, block, row, sub):
    count = len(v)
    line = [spread(v[block][row + i:row + i + 1]) for i in range(4)]
    line_w = [spread(w[block][row + i:row + i + 1]) for i in range(4)] if w else []
    column = {j: [spread(v[j][:, k + i:k + i + 1]) for i in range(4)] for j in range(block, count)}
    p = {(i, h): spread(column[block][i][row + h:row + h + 1]) for i in range(4) for h in range(i, 4)}
    inverse = reciprocal(p[0, 0] * p[1, 1] - p[0, 1] * p[0, 1])
    i00, i01, i11 = p[1, 1] * inverse, -(p[0, 1] * inverse), p[0, 0] * inverse
    f02, f12 = i00 * p[0, 2] + i01 * p[1, 2], i01 * p[0, 2] + i11 * p[1, 2]
    f03, f13 = i00 * p[0, 3] + i01 * p[1, 3], i01 * p[0, 3] + i11 * p[1, 3]
    s22 = p[2, 2] - (p[0, 2] * f02 + p[1, 2] * f12)
    s23 = p[2, 3] - (p[0, 2] * f03 + p[1, 2] * f13)
    s33 = p[3, 3] - (p[0, 3] * f03 + p[1, 3] * f13)
    inverse = reciprocal(s22 * s33 - s23 * s23)
    j22, j23, j33 = s33 * inverse, -(s23 * inverse), s22 * inverse
    f01, f23 = p[0, 1] * reciprocal(p[0, 0]), s23 * reciprocal(s22)
    for lines in (line, line_w)[:2 if w else 1]:
        lines[2] = lines[2] - f02 * lines[0] - f12 * lines[1]
        lines[3] = lines[3] - f03 * lines[0] - f13 * lines[1]
    for j in range(block, count):
        c = column[j]
        if j > block or row == 0:
            g0, g1 = i00 * c[0] + i01 * c[1], i01 * c[0] + i11 * c[1]
            e2 = c[2] - c[0] * f02 - c[1] * f12
            e3 = c[3] - c[0] * f03 - c[1] * f13
            g2, g3 = j22 * e2 + j23 * e3, j23 * e2 + j33 * e3
        else:
            g0 = g1 = g2 = g3 = 0.0
        if j == block:
            inside = jnp.where(sub == row + 1, f01, jnp.where(sub == row + 2, f02, jnp.where(sub == row + 3, f03, 0.0)))
            g0 = jnp.where(sub > row + 3, g0, inside)
            g1 = jnp.where(sub > row + 3, g1, jnp.where(sub == row + 2, f12, jnp.where(sub == row + 3, f13, 0.0)))
            g2 = jnp.where(sub > row + 3, g2, jnp.where(sub == row + 3, f23, 0.0))
            g3 = jnp.where(sub > row + 3, g3, 0.0)
        v[j] = v[j] - g0 * line[0] - g1 * line[1] - g2 * line[2] - g3 * line[3]
        if w:
            w[j] = w[j] - g0 * line_w[0] - g1 * line_w[1] - g2 * line_w[2] - g3 * line_w[3]


def whiten_kernel(levels, rep_ref, *refs):
    x_refs, p_refs, q_refs = refs[:levels], refs[levels:2 * levels], refs[2 * levels:-1]
    out_ref = refs[-1]
    width = x_refs[0].shape[0]
    narrow = out_ref.shape[1]
    lane = lax.broadcasted_iota(jnp.int32, (8, width), 1)
    sub = lax.broadcasted_iota(jnp.int32, (8, width), 0)
    count = PANEL // 8
    lanes = lax.broadcasted_iota(jnp.int32, (width, width), 1)
    state, columns = [], []
    for m in range(levels):
        x, p = x_refs[m][...], p_refs[m]
        p = p[0] if len(p.shape) == 3 else p[...]
        q = q_refs[m - 1][...] if m else identity(width)
        pair = parts(x)
        state.append(q + product(pair, parts(p), ((1,), (1,))) * (1.0 / width))
        columns.append(pltpu.roll(x, width - rep_ref[0] * narrow, 1))
    done = [[] for _ in range(levels)]
    for top in range(0, width, PANEL):
        left = [[s[8 * j:8 * j + 8] for j in range(count)] for s in state]
        right = [[c[8 * j:8 * j + 8] for j in range(count)] if top == 0 else [] for c in columns]
        for kk in range(0, PANEL, 4):
            for m in range(levels):
                eliminate(left[m], right[m], top + kk, kk // 8, kk % 8, sub)
        for m in range(levels):
            for j in range(count):
                diagonal = jnp.sum(jnp.where(lane == sub + (top + 8 * j), left[m][j], 0.0), axis=1, keepdims=True)
                root = lax.rsqrt(diagonal)
                left[m][j] = left[m][j] * root
                if top == 0:
                    right[m][j] = right[m][j] * root
            upper = jnp.concatenate(left[m], axis=0)
            both = upper
            if top == 0:
                both = jnp.where(lanes[:PANEL] < narrow, jnp.concatenate(right[m], axis=0), upper)
            done[m].append(both)
            if top + PANEL < width:
                rest = state[m][PANEL:]
                if top == 0:
                    rest = jnp.where(lanes[PANEL:] < narrow, columns[m][PANEL:], rest)
                state[m] = rest - product(parts(upper.T[top + PANEL:]), parts(both))
    for m in range(levels):
        out_ref[m] = jnp.concatenate(done[m], axis=0).T[:narrow]


def last_kernel(levels, kind, side_ref, core_ref, rep_ref, own_ref, pair_ref, *refs):
    x_refs, p_refs, q_refs = refs[: levels - 1], refs[levels - 1:2 * levels - 1], refs[2 * levels - 1:-2]
    out_ref, x_last = refs[-2:]
    level_kernel(False, True, kind, False, side_ref, core_ref, own_ref, pair_ref, p_refs[-1], x_last)
    whiten_kernel(levels, rep_ref, *x_refs, x_last, *p_refs, *q_refs, out_ref)


def call(kernel, out_shape, n_smem, n_vmem, scratch=()):
    return pl.pallas_call(
        kernel,
        out_shape=out_shape,
        in_specs=[pl.BlockSpec(memory_space=pltpu.SMEM)] * n_smem
        + [pl.BlockSpec(memory_space=pltpu.VMEM)] * n_vmem,
        out_specs=jax.tree.map(lambda _: pl.BlockSpec(memory_space=pltpu.VMEM), out_shape),
        scratch_shapes=list(scratch),
        compiler_params=pltpu.CompilerParams(vmem_limit_bytes=VMEM_BYTES),
    )


def partner(leaf, bit):
    if bit == 0:
        return leaf ^ 1
    if bit == 1:
        return leaf ^ 2
    if bit == 2:
        return leaf ^ 6
    if bit == 4:
        return leaf ^ 24
    if bit == 6:
        z = leaf >> 3
        z = (z + 4) % 16 if z & 4 else (z - 4) % 16
        return z * 8 + (leaf & 7)
    return leaf ^ (1 << bit)


def pair_gathered(value, axis, bit):
    leaves = range(lax.axis_size(axis))
    groups = [[leaf, partner(leaf, bit)] for leaf in leaves if not leaf >> bit & 1]
    return lax.all_gather(value, axis, axis=0, axis_index_groups=groups)


def swapped(value, axis, bit):
    pairs = [(source, partner(source, bit)) for source in range(lax.axis_size(axis))]
    return lax.ppermute(value, axis, pairs)


def local(basis, near_blocks, near_cols, bead_order):
    levels, narrow, rows = basis.shape
    block_rows, per_row = near_cols.shape
    blk = rows // block_rows
    reps = lax.axis_size("rep")
    width = reps * narrow
    leaf_index = lax.axis_index("leaf")
    rep_index = lax.axis_index("rep")
    rep_scalar = rep_index.astype(jnp.int32).reshape(1)
    square = jax.ShapeDtypeStruct((width, width), F32)

    def levels_of(rep):
        return lax.dynamic_slice_in_dim(basis, jnp.maximum(2 * rep - 1, 0), 2, 0)

    pieces = [levels_of(rep_index)]
    for shift in range(1, reps):
        pairs = [(source, (source + shift) % reps) for source in range(reps)]
        pieces.append(lax.ppermute(levels_of(lax.rem(rep_index + shift, reps)), "rep", pairs))
    tiles = near_blocks.reshape(block_rows * per_row, blk, blk)
    dense = [jax.ShapeDtypeStruct((rows, rows), BF16)] * 2
    high, low = call(dense_kernel, dense, 1, 2, [pltpu.VMEM((block_rows, rows, blk), F32)])(
        near_cols, tiles, bead_order
    )
    two = jax.ShapeDtypeStruct((2, width, width), F32)
    mine = call(panel_kernel, two, 1, reps + 2, [pltpu.VMEM((2, width, rows), F32)])(
        rep_scalar, *pieces, high, low
    )
    sent = lax.all_gather(mine, "rep", axis=0, tiled=True)
    core = (leaf_index & 1).astype(jnp.int32).reshape(1)
    half = panel = None
    x_list, p_list, q_list = [], [sent], []
    for bit in range(levels):
        first, last = bit == 0, bit == levels - 1
        kind = EXCHANGE[bit]
        value = half if kind.startswith("half") else sent[1:] if first else sent
        pair = (swapped if kind.endswith("other") else pair_gathered)(value, "leaf", bit)
        if kind.startswith("half"):
            pair = pair_gathered(pair, "leaf", 0)
        side = (leaf_index >> bit & 1).astype(jnp.int32).reshape(1)
        split = not last and EXCHANGE[bit + 1].startswith("half")
        shapes = [square]
        if not last:
            count = levels - bit - 1
            shapes += [square, square, jax.ShapeDtypeStruct((count, width, width), F32)]
            if split:
                shapes.append(jax.ShapeDtypeStruct((count, width // 2, width), F32))
        kernel = functools.partial(level_kernel, first, last, kind, split)
        state = [] if first else [panel]
        if last:
            out = jax.ShapeDtypeStruct((levels, narrow, width), F32)
            kernel = functools.partial(last_kernel, levels, kind)
            return call(kernel, out, 3, 3 * levels, [pltpu.VMEM((width, width), F32)])(
                side, core, rep_scalar, sent, pair, *x_list, *p_list, *q_list
            )
        x, panel, q, sent, *rest = call(kernel, shapes, 2, 2 + len(state))(side, core, sent, pair, *state)
        half = rest[0] if rest else None
        x_list.append(x)
        p_list.append(panel)
        q_list.append(q)


def solution(mesh):
    return jax.shard_map(
        local,
        mesh=mesh,
        in_specs=(P(None, "rep", "leaf"), P("leaf", None, None), P("leaf", None), P("leaf", None)),
        out_specs=P(None, "rep", "leaf"),
        check_vma=False,
    )
```

```python
import functools
import math

import jax
import jax.numpy as jnp
from jax import lax
from jax.experimental import pallas as pl
from jax.experimental.pallas import tpu as pltpu
from jax.sharding import PartitionSpec as P

F32 = jnp.float32
BF16 = jnp.bfloat16
PANEL = 32
EXCHANGE = ("pair",) * 7
VMEM_BYTES = 48 * 1024 * 1024


def parts(x):
    high = x.astype(BF16)
    return high, (x - high.astype(F32)).astype(BF16)


def contract(a, b, dims):
    return lax.dot_general(a, b, (dims, ((), ())), preferred_element_type=F32)


def product(a, b, dims=((1,), (0,))):
    return contract(a[0], b[0], dims) + (contract(a[0], b[1], dims) + contract(a[1], b[0], dims))


def wide_product(a, b, dims=((1,), (0,))):
    (ca,), (cb,) = dims
    above = jnp.concatenate([b[0], b[1]], axis=1 - cb)
    below = jnp.concatenate([b[0], jnp.zeros_like(b[1])], axis=1 - cb)
    both = contract(jnp.concatenate([a[0], a[1]], axis=ca), jnp.concatenate([above, below], axis=cb), dims)
    half = both.shape[1] // 2
    return both[:, :half] + both[:, half:]


def identity(n):
    rows = lax.broadcasted_iota(jnp.int32, (n, n), 0)
    return (rows == lax.broadcasted_iota(jnp.int32, (n, n), 1)).astype(F32)


def dense_kernel(cols_ref, blocks_ref, order_ref, high_ref, low_ref, columns):
    block_rows, per_row = cols_ref.shape
    blk = blocks_ref.shape[1]
    rows = block_rows * blk
    columns[...] = jnp.zeros_like(columns)
    for q in range(block_rows):
        for n in range(per_row):
            where = (cols_ref[q, n], slice(q * blk, (q + 1) * blk))
            columns[where] = columns[where] + blocks_ref[q * per_row + n]
    tree = jnp.concatenate([columns[c] for c in range(block_rows)], axis=1)
    bead = lax.broadcasted_iota(jnp.int32, (rows, rows), 0)
    select = (bead == order_ref[...]).astype(F32).astype(BF16)
    for piece, out in zip(parts(tree), (high_ref, low_ref)):
        moved = contract(select, piece, ((1,), (0,))).astype(BF16)
        out[...] = contract(moved, select, ((1,), (1,))).astype(BF16)


def panel_kernel(rep_ref, own_ref, *refs):
    reps = len(refs) - 3
    pieces, (high_ref, low_ref, out_ref, basis_scr) = (own_ref, *refs[: reps - 1]), refs[reps - 1:]
    own_levels, narrow, rows = own_ref.shape
    scale = 1.0 / math.sqrt(rows)
    width = reps * narrow
    rep = rep_ref[0]
    for shift, piece in enumerate(pieces):
        source = lax.rem(rep + reps - shift, reps)
        basis_scr[:, pl.ds(pl.multiple_of(source * narrow, narrow), narrow), :] = piece[...]
    panels = []
    for level in range(own_levels):
        basis = parts(basis_scr[level])
        image = product(basis, (high_ref[...], low_ref[...]))
        panels.append(product(parts(image), basis, ((1,), (1,))) * scale)
    pair = parts(panels[0])
    first = product(pair, pair, ((0,), (0,))) * (1.0 / width)
    out_ref[0] = panels[0]
    out_ref[1] = jnp.where(rep == 0, first, panels[1])


def level_kernel(first, last, kind, split, side_ref, core_ref, own_ref, pair_ref, *refs):
    width = own_ref.shape[1]
    eye = identity(width)
    side = side_ref[0]
    skip = 1 if first else 0
    if first:
        panel, outs = own_ref[0], refs
    else:
        panel, outs = refs[0][...], refs[1:]

    def theirs(n):
        if kind == "other":
            return pair_ref[n]
        if kind == "pair":
            return pair_ref[1 - side, n]
        if kind == "halfother":
            return jnp.concatenate([pair_ref[core, n] for core in range(2)], axis=0)
        return jnp.concatenate([pair_ref[core, 1 - side, n] for core in range(2)], axis=0)

    def ours(n):
        return own_ref[n + skip]

    own, other = ours(0), theirs(0)
    total = own + other
    bound = 1.0 + 2.0 * jnp.max(jnp.sum(jnp.abs(total), axis=0))
    if last:
        matrices = [eye + other]
    else:
        matrices = [eye + other, eye + total, eye + 2.0 * total]
        root_half = math.sqrt(0.5)
        next_panel = (ours(1) + theirs(1)) * root_half
    step = 2.0 / (bound + 1.0)
    rho = 1.0 - step
    scale = 2.0 / (2.0 - rho * rho)
    begun = []
    for matrix in matrices:
        residual = eye - step * matrix
        e = parts(residual)
        begun.append(((scale * step) * (eye + residual), (1.0 - scale) * eye + scale * wide_product(e, e)))
    start = (0.5 * scale * rho * rho, tuple(begun))

    def go_on(carry):
        return carry[0] > 1e-2

    def refine(carry):
        rho, inverses = carry
        scale = 2.0 / (2.0 - rho * rho)
        new = []
        for inverse, residual in inverses:
            e = parts(residual)
            better = scale * (inverse + wide_product(parts(inverse), e))
            new.append((better, (1.0 - scale) * eye + scale * wide_product(e, e)))
        return (0.5 * scale * rho * rho, tuple(new))

    _, inverses = lax.while_loop(go_on, refine, start)
    pairs = [parts(matrix) for matrix in matrices]

    def correct(_, found):
        new = []
        for inverse, pair in zip(found, pairs):
            x = parts(inverse)
            new.append(inverse + wide_product(x, parts(eye - wide_product(pair, x))))
        return tuple(new)

    extra = jnp.where(bound > 200.0, 3, 0)
    inverses = lax.fori_loop(0, extra, correct, tuple(inverse for inverse, _ in inverses))
    x = [parts(inverse) for inverse in inverses]
    residuals = [parts(eye - wide_product(pair, inverse)) for pair, inverse in zip(pairs, x)]
    if not last:
        next_panel_ref, next_q_ref, next_ref = outs[1:4]
        p = parts(next_panel)
        r = residuals[2]
        y = wide_product(x[2], p)
        ry, rp = wide_product(r, parts(y)), wide_product(r, p)
        sum_y = next_panel + y
        plain = wide_product(p, parts(sum_y), ((0,), (0,)))
        bent = wide_product(parts(ry), parts(next_panel + rp), ((0,), (0,)))
        next_ref[0] = (plain + bent) * (0.5 / width)
        next_panel_ref[...] = next_panel
        for upper in range(1, next_ref.shape[0]):
            next_ref[upper] = (ours(upper + 1) + theirs(upper + 1)) * root_half
        if split:
            half_rows = width // 2
            outs[4][...] = next_ref[:, pl.ds(pl.multiple_of(core_ref[0] * half_rows, half_rows), half_rows), :]
        r = residuals[1]
        both = eye - wide_product(pairs[1], x[1]) + wide_product(r, r)
        next_q_ref[...] = 2.0 * eye - (inverses[1] + wide_product(x[1], parts(both)))
    r = residuals[0]
    v = wide_product(parts(panel), x[0])
    vr = wide_product(parts(v), r)
    gained = v + vr + wide_product(parts(vr), r)
    outs[0][...] = jnp.where(side == 1, gained, panel)


def spread(x):
    return jnp.broadcast_to(x, (8, 128))


def reciprocal(x):
    guess = pl.reciprocal(x, approx=True)
    return guess * (2.0 - x * guess)


def eliminate(v, w, k, block, row, sub, area):
    count = len(v)
    area[0] = v[block]
    line = [spread(area[0, row + i:row + i + 1, :]) for i in range(4)]
    line_w = []
    if w:
        area[1] = w[block]
        line_w = [spread(area[1, row + i:row + i + 1, :]) for i in range(4)]
    column = {j: [spread(v[j][:, k + i:k + i + 1]) for i in range(4)] for j in range(block, count)}
    for i in range(4):
        area[2 + i] = column[block][i]
    p = {(i, h): spread(area[2 + i, row + h:row + h + 1, :]) for i in range(4) for h in range(i, 4)}
    inverse = reciprocal(p[0, 0] * p[1, 1] - p[0, 1] * p[0, 1])
    i00, i01, i11 = p[1, 1] * inverse, -(p[0, 1] * inverse), p[0, 0] * inverse
    f02, f12 = i00 * p[0, 2] + i01 * p[1, 2], i01 * p[0, 2] + i11 * p[1, 2]
    f03, f13 = i00 * p[0, 3] + i01 * p[1, 3], i01 * p[0, 3] + i11 * p[1, 3]
    s22 = p[2, 2] - (p[0, 2] * f02 + p[1, 2] * f12)
    s23 = p[2, 3] - (p[0, 2] * f03 + p[1, 2] * f13)
    s33 = p[3, 3] - (p[0, 3] * f03 + p[1, 3] * f13)
    inverse = reciprocal(s22 * s33 - s23 * s23)
    j22, j23, j33 = s33 * inverse, -(s23 * inverse), s22 * inverse
    f01, f23 = p[0, 1] * reciprocal(p[0, 0]), s23 * reciprocal(s22)
    for lines in (line, line_w)[:2 if w else 1]:
        lines[2] = lines[2] - f02 * lines[0] - f12 * lines[1]
        lines[3] = lines[3] - f03 * lines[0] - f13 * lines[1]
    for j in range(block, count):
        c = column[j]
        if j > block or row == 0:
            g0, g1 = i00 * c[0] + i01 * c[1], i01 * c[0] + i11 * c[1]
            e2 = c[2] - c[0] * f02 - c[1] * f12
            e3 = c[3] - c[0] * f03 - c[1] * f13
            g2, g3 = j22 * e2 + j23 * e3, j23 * e2 + j33 * e3
        else:
            g0 = g1 = g2 = g3 = 0.0
        if j == block:
            inside = jnp.where(sub == row + 1, f01, jnp.where(sub == row + 2, f02, jnp.where(sub == row + 3, f03, 0.0)))
            g0 = jnp.where(sub > row + 3, g0, inside)
            g1 = jnp.where(sub > row + 3, g1, jnp.where(sub == row + 2, f12, jnp.where(sub == row + 3, f13, 0.0)))
            g2 = jnp.where(sub > row + 3, g2, jnp.where(sub == row + 3, f23, 0.0))
            g3 = jnp.where(sub > row + 3, g3, 0.0)
        v[j] = v[j] - g0 * line[0] - g1 * line[1] - g2 * line[2] - g3 * line[3]
        if w:
            w[j] = w[j] - g0 * line_w[0] - g1 * line_w[1] - g2 * line_w[2] - g3 * line_w[3]


def whiten_kernel(levels, area, rep_ref, *refs):
    x_refs, p_refs, q_refs = refs[:levels], refs[levels:2 * levels], refs[2 * levels:-1]
    out_ref = refs[-1]
    width = x_refs[0].shape[0]
    narrow = out_ref.shape[1]
    lane = lax.broadcasted_iota(jnp.int32, (8, width), 1)
    sub = lax.broadcasted_iota(jnp.int32, (8, width), 0)
    count = PANEL // 8
    lanes = lax.broadcasted_iota(jnp.int32, (width, width), 1)
    state, columns = [], []
    for m in range(levels):
        x, p = x_refs[m][...], p_refs[m]
        p = p[0] if len(p.shape) == 3 else p[...]
        q = q_refs[m - 1][...] if m else identity(width)
        pair = parts(x)
        state.append(q + product(pair, parts(p), ((1,), (1,))) * (1.0 / width))
        columns.append(pltpu.roll(x, width - rep_ref[0] * narrow, 1))
    done = [[] for _ in range(levels)]
    for top in range(0, width, PANEL):
        left = [[s[8 * j:8 * j + 8] for j in range(count)] for s in state]
        right = [[c[8 * j:8 * j + 8] for j in range(count)] if top == 0 else [] for c in columns]
        for kk in range(0, PANEL, 4):
            for m in range(levels):
                eliminate(left[m], right[m], top + kk, kk // 8, kk % 8, sub, area.at[m, kk // 4 % 2])
        for m in range(levels):
            for j in range(count):
                diagonal = jnp.sum(jnp.where(lane == sub + (top + 8 * j), left[m][j], 0.0), axis=1, keepdims=True)
                root = lax.rsqrt(diagonal)
                left[m][j] = left[m][j] * root
                if top == 0:
                    right[m][j] = right[m][j] * root
            upper = jnp.concatenate(left[m], axis=0)
            both = upper
            if top == 0:
                both = jnp.where(lanes[:PANEL] < narrow, jnp.concatenate(right[m], axis=0), upper)
            done[m].append(both)
            if top + PANEL < width:
                rest = state[m][PANEL:]
                if top == 0:
                    rest = jnp.where(lanes[PANEL:] < narrow, columns[m][PANEL:], rest)
                state[m] = rest - product(parts(upper.T[top + PANEL:]), parts(both))
    for m in range(levels):
        out_ref[m] = jnp.concatenate(done[m], axis=0).T[:narrow]


def last_kernel(levels, kind, side_ref, core_ref, rep_ref, own_ref, pair_ref, *refs):
    x_refs, p_refs, q_refs = refs[: levels - 1], refs[levels - 1:2 * levels - 1], refs[2 * levels - 1:-3]
    out_ref, x_last, area = refs[-3:]
    level_kernel(False, True, kind, False, side_ref, core_ref, own_ref, pair_ref, p_refs[-1], x_last)
    whiten_kernel(levels, area, rep_ref, *x_refs, x_last, *p_refs, *q_refs, out_ref)


def call(kernel, out_shape, n_smem, n_vmem, scratch=()):
    return pl.pallas_call(
        kernel,
        out_shape=out_shape,
        in_specs=[pl.BlockSpec(memory_space=pltpu.SMEM)] * n_smem
        + [pl.BlockSpec(memory_space=pltpu.VMEM)] * n_vmem,
        out_specs=jax.tree.map(lambda _: pl.BlockSpec(memory_space=pltpu.VMEM), out_shape),
        scratch_shapes=list(scratch),
        compiler_params=pltpu.CompilerParams(vmem_limit_bytes=VMEM_BYTES),
    )


def partner(leaf, bit):
    if bit == 0:
        return leaf ^ 1
    if bit == 1:
        return leaf ^ 2
    if bit == 2:
        return leaf ^ 6
    if bit == 4:
        return leaf ^ 24
    if bit == 6:
        z = leaf >> 3
        z = (z + 4) % 16 if z & 4 else (z - 4) % 16
        return z * 8 + (leaf & 7)
    return leaf ^ (1 << bit)


def pair_gathered(value, axis, bit):
    leaves = range(lax.axis_size(axis))
    groups = [[leaf, partner(leaf, bit)] for leaf in leaves if not leaf >> bit & 1]
    return lax.all_gather(value, axis, axis=0, axis_index_groups=groups)


def swapped(value, axis, bit):
    pairs = [(source, partner(source, bit)) for source in range(lax.axis_size(axis))]
    return lax.ppermute(value, axis, pairs)


def local(basis, near_blocks, near_cols, bead_order):
    levels, narrow, rows = basis.shape
    block_rows, per_row = near_cols.shape
    blk = rows // block_rows
    reps = lax.axis_size("rep")
    width = reps * narrow
    leaf_index = lax.axis_index("leaf")
    rep_index = lax.axis_index("rep")
    rep_scalar = rep_index.astype(jnp.int32).reshape(1)
    square = jax.ShapeDtypeStruct((width, width), F32)

    def levels_of(rep):
        return lax.dynamic_slice_in_dim(basis, jnp.maximum(2 * rep - 1, 0), 2, 0)

    pieces = [levels_of(rep_index)]
    for shift in range(1, reps):
        pairs = [(source, (source + shift) % reps) for source in range(reps)]
        pieces.append(lax.ppermute(levels_of(lax.rem(rep_index + shift, reps)), "rep", pairs))
    tiles = near_blocks.reshape(block_rows * per_row, blk, blk)
    dense = [jax.ShapeDtypeStruct((rows, rows), BF16)] * 2
    high, low = call(dense_kernel, dense, 1, 2, [pltpu.VMEM((block_rows, rows, blk), F32)])(
        near_cols, tiles, bead_order
    )
    two = jax.ShapeDtypeStruct((2, width, width), F32)
    mine = call(panel_kernel, two, 1, reps + 2, [pltpu.VMEM((2, width, rows), F32)])(
        rep_scalar, *pieces, high, low
    )
    sent = lax.all_gather(mine, "rep", axis=0, tiled=True)
    core = (leaf_index & 1).astype(jnp.int32).reshape(1)
    half = panel = None
    x_list, p_list, q_list = [], [sent], []
    for bit in range(levels):
        first, last = bit == 0, bit == levels - 1
        kind = EXCHANGE[bit]
        value = half if kind.startswith("half") else sent[1:] if first else sent
        pair = (swapped if kind.endswith("other") else pair_gathered)(value, "leaf", bit)
        if kind.startswith("half"):
            pair = pair_gathered(pair, "leaf", 0)
        side = (leaf_index >> bit & 1).astype(jnp.int32).reshape(1)
        split = not last and EXCHANGE[bit + 1].startswith("half")
        shapes = [square]
        if not last:
            count = levels - bit - 1
            shapes += [square, square, jax.ShapeDtypeStruct((count, width, width), F32)]
            if split:
                shapes.append(jax.ShapeDtypeStruct((count, width // 2, width), F32))
        kernel = functools.partial(level_kernel, first, last, kind, split)
        state = [] if first else [panel]
        if last:
            out = jax.ShapeDtypeStruct((levels, narrow, width), F32)
            kernel = functools.partial(last_kernel, levels, kind)
            scratch = [pltpu.VMEM((width, width), F32), pltpu.VMEM((levels, 2, 6, 8, width), F32)]
            return call(kernel, out, 3, 3 * levels, scratch)(
                side, core, rep_scalar, sent, pair, *x_list, *p_list, *q_list
            )
        x, panel, q, sent, *rest = call(kernel, shapes, 2, 2 + len(state))(side, core, sent, pair, *state)
        half = rest[0] if rest else None
        x_list.append(x)
        p_list.append(panel)
        q_list.append(q)


def solution(mesh):
    return jax.shard_map(
        local,
        mesh=mesh,
        in_specs=(P(None, "rep", "leaf"), P("leaf", None, None), P("leaf", None), P("leaf", None)),
        out_specs=P(None, "rep", "leaf"),
        check_vma=False,
    )
```

```python
import functools
import math

import jax
import jax.numpy as jnp
from jax import lax
from jax.experimental import pallas as pl
from jax.experimental.pallas import tpu as pltpu
from jax.sharding import PartitionSpec as P

F32 = jnp.float32
BF16 = jnp.bfloat16
PANEL = 32
EXCHANGE = ("pair",) * 7
VMEM_BYTES = 48 * 1024 * 1024


def parts(x):
    high = x.astype(BF16)
    return high, (x - high.astype(F32)).astype(BF16)


def contract(a, b, dims):
    return lax.dot_general(a, b, (dims, ((), ())), preferred_element_type=F32)


def product(a, b, dims=((1,), (0,))):
    return contract(a[0], b[0], dims) + (contract(a[0], b[1], dims) + contract(a[1], b[0], dims))


def wide_product(a, b, dims=((1,), (0,))):
    (ca,), (cb,) = dims
    above = jnp.concatenate([b[0], b[1]], axis=1 - cb)
    below = jnp.concatenate([b[0], jnp.zeros_like(b[1])], axis=1 - cb)
    both = contract(jnp.concatenate([a[0], a[1]], axis=ca), jnp.concatenate([above, below], axis=cb), dims)
    half = both.shape[1] // 2
    return both[:, :half] + both[:, half:]


def first_level(rep):
    return jnp.maximum(2 * rep - 1, 0)


def identity(n):
    rows = lax.broadcasted_iota(jnp.int32, (n, n), 0)
    return (rows == lax.broadcasted_iota(jnp.int32, (n, n), 1)).astype(F32)


def dense_kernel(cols_ref, blocks_ref, order_ref, high_ref, low_ref, select_ref, columns):
    block_rows, per_row = cols_ref.shape
    blk = blocks_ref.shape[1]
    rows = block_rows * blk
    columns[...] = jnp.zeros_like(columns)
    for q in range(block_rows):
        for n in range(per_row):
            where = (cols_ref[q, n], slice(q * blk, (q + 1) * blk))
            columns[where] = columns[where] + blocks_ref[q * per_row + n]
    high_ref[...], low_ref[...] = parts(jnp.concatenate([columns[c] for c in range(block_rows)], axis=1))
    bead = lax.broadcasted_iota(jnp.int32, (rows, rows), 0)
    select_ref[...] = (bead == order_ref[...]).astype(F32).astype(BF16)


def panel_kernel(rep_ref, basis_ref, *refs):
    narrow, rows = basis_ref.shape[1:]
    pieces, (high_ref, low_ref, select_ref, out_ref, basis_scr) = refs[:-5], refs[-5:]
    reps = len(pieces) + 1
    own_levels = out_ref.shape[0]
    scale = 1.0 / math.sqrt(rows)
    width = reps * narrow
    rep = rep_ref[0]
    for shift in range(reps):
        source = lax.rem(rep + reps - shift, reps)
        piece = pieces[shift - 1][...] if shift else basis_ref[pl.ds(first_level(rep), own_levels)]
        basis_scr[:, pl.ds(pl.multiple_of(source * narrow, narrow), narrow), :] = piece
    panels = []
    for level in range(own_levels):
        ordered = tuple(contract(piece, select_ref[...], ((1,), (0,))).astype(BF16) for piece in parts(basis_scr[level]))
        image = product(ordered, (high_ref[...], low_ref[...]))
        panels.append(product(parts(image), ordered, ((1,), (1,))) * scale)
    pair = parts(panels[0])
    first = product(pair, pair, ((0,), (0,))) * (1.0 / width)
    out_ref[0] = panels[0]
    out_ref[1] = jnp.where(rep == 0, first, panels[1])


def level_kernel(first, last, kind, split, side_ref, core_ref, own_ref, pair_ref, *refs):
    width = own_ref.shape[1]
    eye = identity(width)
    side = side_ref[0]
    skip = 1 if first else 0
    if first:
        panel, outs = own_ref[0], refs
    else:
        panel, outs = refs[0][...], refs[1:]

    def theirs(n):
        if kind == "other":
            return pair_ref[n]
        if kind == "pair":
            return pair_ref[1 - side, n]
        if kind == "halfother":
            return jnp.concatenate([pair_ref[core, n] for core in range(2)], axis=0)
        return jnp.concatenate([pair_ref[core, 1 - side, n] for core in range(2)], axis=0)

    def ours(n):
        return own_ref[n + skip]

    own, other = ours(0), theirs(0)
    total = own + other
    bound = 1.0 + 2.0 * jnp.max(jnp.sum(jnp.abs(total), axis=0))
    if last:
        matrices = [eye + other]
    else:
        matrices = [eye + other, eye + total, eye + 2.0 * total]
        root_half = math.sqrt(0.5)
        next_panel = (ours(1) + theirs(1)) * root_half
    step = 2.0 / (bound + 1.0)
    rho = 1.0 - step
    scale = 2.0 / (2.0 - rho * rho)
    begun = []
    for matrix in matrices:
        residual = eye - step * matrix
        e = parts(residual)
        begun.append(((scale * step) * (eye + residual), (1.0 - scale) * eye + scale * wide_product(e, e)))
    start = (0.5 * scale * rho * rho, tuple(begun))

    def go_on(carry):
        return carry[0] > 1e-2

    def refine(carry):
        rho, inverses = carry
        scale = 2.0 / (2.0 - rho * rho)
        new = []
        for inverse, residual in inverses:
            e = parts(residual)
            better = scale * (inverse + wide_product(parts(inverse), e))
            new.append((better, (1.0 - scale) * eye + scale * wide_product(e, e)))
        return (0.5 * scale * rho * rho, tuple(new))

    _, inverses = lax.while_loop(go_on, refine, start)
    pairs = [parts(matrix) for matrix in matrices]

    def correct(_, found):
        new = []
        for inverse, pair in zip(found, pairs):
            x = parts(inverse)
            new.append(inverse + wide_product(x, parts(eye - wide_product(pair, x))))
        return tuple(new)

    extra = jnp.where(bound > 200.0, 3, 0)
    inverses = lax.fori_loop(0, extra, correct, tuple(inverse for inverse, _ in inverses))
    x = [parts(inverse) for inverse in inverses]
    residuals = [parts(eye - wide_product(pair, inverse)) for pair, inverse in zip(pairs, x)]
    if not last:
        next_panel_ref, next_q_ref, next_ref = outs[1:4]
        p = parts(next_panel)
        r = residuals[2]
        y = wide_product(x[2], p)
        ry, rp = wide_product(r, parts(y)), wide_product(r, p)
        sum_y = next_panel + y
        plain = wide_product(p, parts(sum_y), ((0,), (0,)))
        bent = wide_product(parts(ry), parts(next_panel + rp), ((0,), (0,)))
        next_ref[0] = (plain + bent) * (0.5 / width)
        next_panel_ref[...] = next_panel
        for upper in range(1, next_ref.shape[0]):
            next_ref[upper] = (ours(upper + 1) + theirs(upper + 1)) * root_half
        if split:
            half_rows = width // 2
            outs[4][...] = next_ref[:, pl.ds(pl.multiple_of(core_ref[0] * half_rows, half_rows), half_rows), :]
        r = residuals[1]
        both = eye - wide_product(pairs[1], x[1]) + wide_product(r, r)
        next_q_ref[...] = 2.0 * eye - (inverses[1] + wide_product(x[1], parts(both)))
    r = residuals[0]
    v = wide_product(parts(panel), x[0])
    vr = wide_product(parts(v), r)
    gained = v + vr + wide_product(parts(vr), r)
    outs[0][...] = jnp.where(side == 1, gained, panel)


def spread(x):
    return jnp.broadcast_to(x, (8, 128))


def reciprocal(x):
    guess = pl.reciprocal(x, approx=True)
    return guess * (2.0 - x * guess)


def eliminate(v, w, k, block, row, sub, area):
    count = len(v)
    area[0] = v[block]
    line = [spread(area[0, row + i:row + i + 1, :]) for i in range(4)]
    line_w = []
    if w:
        area[1] = w[block]
        line_w = [spread(area[1, row + i:row + i + 1, :]) for i in range(4)]
    column = {j: [spread(v[j][:, k + i:k + i + 1]) for i in range(4)] for j in range(block, count)}
    for i in range(4):
        area[2 + i] = column[block][i]
    p = {(i, h): spread(area[2 + i, row + h:row + h + 1, :]) for i in range(4) for h in range(i, 4)}
    inverse = reciprocal(p[0, 0] * p[1, 1] - p[0, 1] * p[0, 1])
    i00, i01, i11 = p[1, 1] * inverse, -(p[0, 1] * inverse), p[0, 0] * inverse
    f02, f12 = i00 * p[0, 2] + i01 * p[1, 2], i01 * p[0, 2] + i11 * p[1, 2]
    f03, f13 = i00 * p[0, 3] + i01 * p[1, 3], i01 * p[0, 3] + i11 * p[1, 3]
    s22 = p[2, 2] - (p[0, 2] * f02 + p[1, 2] * f12)
    s23 = p[2, 3] - (p[0, 2] * f03 + p[1, 2] * f13)
    s33 = p[3, 3] - (p[0, 3] * f03 + p[1, 3] * f13)
    inverse = reciprocal(s22 * s33 - s23 * s23)
    j22, j23, j33 = s33 * inverse, -(s23 * inverse), s22 * inverse
    f01, f23 = p[0, 1] * reciprocal(p[0, 0]), s23 * reciprocal(s22)
    for lines in (line, line_w)[:2 if w else 1]:
        lines[2] = lines[2] - f02 * lines[0] - f12 * lines[1]
        lines[3] = lines[3] - f03 * lines[0] - f13 * lines[1]
    for j in range(block, count):
        c = column[j]
        if j > block or row == 0:
            g0, g1 = i00 * c[0] + i01 * c[1], i01 * c[0] + i11 * c[1]
            e2 = c[2] - c[0] * f02 - c[1] * f12
            e3 = c[3] - c[0] * f03 - c[1] * f13
            g2, g3 = j22 * e2 + j23 * e3, j23 * e2 + j33 * e3
        else:
            g0 = g1 = g2 = g3 = 0.0
        if j == block:
            inside = jnp.where(sub == row + 1, f01, jnp.where(sub == row + 2, f02, jnp.where(sub == row + 3, f03, 0.0)))
            g0 = jnp.where(sub > row + 3, g0, inside)
            g1 = jnp.where(sub > row + 3, g1, jnp.where(sub == row + 2, f12, jnp.where(sub == row + 3, f13, 0.0)))
            g2 = jnp.where(sub > row + 3, g2, jnp.where(sub == row + 3, f23, 0.0))
            g3 = jnp.where(sub > row + 3, g3, 0.0)
        v[j] = v[j] - g0 * line[0] - g1 * line[1] - g2 * line[2] - g3 * line[3]
        if w:
            w[j] = w[j] - g0 * line_w[0] - g1 * line_w[1] - g2 * line_w[2] - g3 * line_w[3]


def whiten_kernel(levels, area, rep_ref, *refs):
    x_refs, p_refs, q_refs = refs[:levels], refs[levels:2 * levels], refs[2 * levels:-1]
    out_ref = refs[-1]
    width = x_refs[0].shape[0]
    narrow = out_ref.shape[1]
    lane = lax.broadcasted_iota(jnp.int32, (8, width), 1)
    sub = lax.broadcasted_iota(jnp.int32, (8, width), 0)
    count = PANEL // 8
    lanes = lax.broadcasted_iota(jnp.int32, (width, width), 1)
    state, columns = [], []
    for m in range(levels):
        x, p = x_refs[m][...], p_refs[m]
        p = p[0] if len(p.shape) == 3 else p[...]
        q = q_refs[m - 1][...] if m else identity(width)
        pair = parts(x)
        state.append(q + product(pair, parts(p), ((1,), (1,))) * (1.0 / width))
        columns.append(pltpu.roll(x, width - rep_ref[0] * narrow, 1))
    done = [[] for _ in range(levels)]
    for top in range(0, width, PANEL):
        left = [[s[8 * j:8 * j + 8] for j in range(count)] for s in state]
        right = [[c[8 * j:8 * j + 8] for j in range(count)] if top == 0 else [] for c in columns]
        for kk in range(0, PANEL, 4):
            for m in range(levels):
                eliminate(left[m], right[m], top + kk, kk // 8, kk % 8, sub, area.at[m, kk // 4 % 2])
        for m in range(levels):
            for j in range(count):
                diagonal = jnp.sum(jnp.where(lane == sub + (top + 8 * j), left[m][j], 0.0), axis=1, keepdims=True)
                root = lax.rsqrt(diagonal)
                left[m][j] = left[m][j] * root
                if top == 0:
                    right[m][j] = right[m][j] * root
            upper = jnp.concatenate(left[m], axis=0)
            both = upper
            if top == 0:
                both = jnp.where(lanes[:PANEL] < narrow, jnp.concatenate(right[m], axis=0), upper)
            done[m].append(both)
            if top + PANEL < width:
                rest = state[m][PANEL:]
                if top == 0:
                    rest = jnp.where(lanes[PANEL:] < narrow, columns[m][PANEL:], rest)
                state[m] = rest - product(parts(upper.T[top + PANEL:]), parts(both))
    for m in range(levels):
        out_ref[m] = jnp.concatenate(done[m], axis=0).T[:narrow]


def last_kernel(levels, kind, side_ref, core_ref, rep_ref, own_ref, pair_ref, *refs):
    x_refs, p_refs, q_refs = refs[: levels - 1], refs[levels - 1:2 * levels - 1], refs[2 * levels - 1:-3]
    out_ref, x_last, area = refs[-3:]
    level_kernel(False, True, kind, False, side_ref, core_ref, own_ref, pair_ref, p_refs[-1], x_last)
    whiten_kernel(levels, area, rep_ref, *x_refs, x_last, *p_refs, *q_refs, out_ref)


def call(kernel, out_shape, n_smem, n_vmem, scratch=()):
    return pl.pallas_call(
        kernel,
        out_shape=out_shape,
        in_specs=[pl.BlockSpec(memory_space=pltpu.SMEM)] * n_smem
        + [pl.BlockSpec(memory_space=pltpu.VMEM)] * n_vmem,
        out_specs=jax.tree.map(lambda _: pl.BlockSpec(memory_space=pltpu.VMEM), out_shape),
        scratch_shapes=list(scratch),
        compiler_params=pltpu.CompilerParams(vmem_limit_bytes=VMEM_BYTES),
    )


def partner(leaf, bit):
    if bit == 0:
        return leaf ^ 1
    if bit == 1:
        return leaf ^ 2
    if bit == 2:
        return leaf ^ 6
    if bit == 4:
        return leaf ^ 24
    if bit == 6:
        z = leaf >> 3
        z = (z + 4) % 16 if z & 4 else (z - 4) % 16
        return z * 8 + (leaf & 7)
    return leaf ^ (1 << bit)


def pair_gathered(value, axis, bit):
    leaves = range(lax.axis_size(axis))
    groups = [[leaf, partner(leaf, bit)] for leaf in leaves if not leaf >> bit & 1]
    return lax.all_gather(value, axis, axis=0, axis_index_groups=groups)


def swapped(value, axis, bit):
    pairs = [(source, partner(source, bit)) for source in range(lax.axis_size(axis))]
    return lax.ppermute(value, axis, pairs)


def local(basis, near_blocks, near_cols, bead_order):
    levels, narrow, rows = basis.shape
    block_rows, per_row = near_cols.shape
    blk = rows // block_rows
    reps = lax.axis_size("rep")
    width = reps * narrow
    leaf_index = lax.axis_index("leaf")
    rep_index = lax.axis_index("rep")
    rep_scalar = rep_index.astype(jnp.int32).reshape(1)
    square = jax.ShapeDtypeStruct((width, width), F32)

    def levels_of(rep):
        return lax.dynamic_slice_in_dim(basis, first_level(rep), 2, 0)

    pieces = []
    for shift in range(1, reps):
        pairs = [(source, (source + shift) % reps) for source in range(reps)]
        pieces.append(lax.ppermute(levels_of(lax.rem(rep_index + shift, reps)), "rep", pairs))
    tiles = near_blocks.reshape(block_rows * per_row, blk, blk)
    dense = [jax.ShapeDtypeStruct((rows, rows), BF16)] * 3
    near = call(dense_kernel, dense, 1, 2, [pltpu.VMEM((block_rows, rows, blk), F32)])(
        near_cols, tiles, bead_order
    )
    two = jax.ShapeDtypeStruct((2, width, width), F32)
    mine = call(panel_kernel, two, 1, reps + 3, [pltpu.VMEM((2, width, rows), F32)])(
        rep_scalar, basis, *pieces, *near
    )
    sent = lax.all_gather(mine, "rep", axis=0, tiled=True)
    core = (leaf_index & 1).astype(jnp.int32).reshape(1)
    half = panel = None
    x_list, p_list, q_list = [], [sent], []
    for bit in range(levels):
        first, last = bit == 0, bit == levels - 1
        kind = EXCHANGE[bit]
        value = half if kind.startswith("half") else sent[1:] if first else sent
        pair = (swapped if kind.endswith("other") else pair_gathered)(value, "leaf", bit)
        if kind.startswith("half"):
            pair = pair_gathered(pair, "leaf", 0)
        side = (leaf_index >> bit & 1).astype(jnp.int32).reshape(1)
        split = not last and EXCHANGE[bit + 1].startswith("half")
        shapes = [square]
        if not last:
            count = levels - bit - 1
            shapes += [square, square, jax.ShapeDtypeStruct((count, width, width), F32)]
            if split:
                shapes.append(jax.ShapeDtypeStruct((count, width // 2, width), F32))
        kernel = functools.partial(level_kernel, first, last, kind, split)
        state = [] if first else [panel]
        if last:
            out = jax.ShapeDtypeStruct((levels, narrow, width), F32)
            kernel = functools.partial(last_kernel, levels, kind)
            scratch = [pltpu.VMEM((width, width), F32), pltpu.VMEM((levels, 2, 6, 8, width), F32)]
            return call(kernel, out, 3, 3 * levels, scratch)(
                side, core, rep_scalar, sent, pair, *x_list, *p_list, *q_list
            )
        x, panel, q, sent, *rest = call(kernel, shapes, 2, 2 + len(state))(side, core, sent, pair, *state)
        half = rest[0] if rest else None
        x_list.append(x)
        p_list.append(panel)
        q_list.append(q)


def solution(mesh):
    return jax.shard_map(
        local,
        mesh=mesh,
        in_specs=(P(None, "rep", "leaf"), P("leaf", None, None), P("leaf", None), P("leaf", None)),
        out_specs=P(None, "rep", "leaf"),
        check_vma=False,
    )
```

```python
import functools
import math

import jax
import jax.numpy as jnp
from jax import lax
from jax.experimental import pallas as pl
from jax.experimental.pallas import tpu as pltpu
from jax.sharding import PartitionSpec as P

F32 = jnp.float32
BF16 = jnp.bfloat16
PANEL = 32
EXCHANGE = ("pair",) * 5 + ("packed", "packed")
VMEM_BYTES = 48 * 1024 * 1024


def parts(x):
    high = x.astype(BF16)
    return high, (x - high.astype(F32)).astype(BF16)


def contract(a, b, dims):
    return lax.dot_general(a, b, (dims, ((), ())), preferred_element_type=F32)


def product(a, b, dims=((1,), (0,))):
    return contract(a[0], b[0], dims) + (contract(a[0], b[1], dims) + contract(a[1], b[0], dims))


def wide_product(a, b, dims=((1,), (0,))):
    (ca,), (cb,) = dims
    above = jnp.concatenate([b[0], b[1]], axis=1 - cb)
    below = jnp.concatenate([b[0], jnp.zeros_like(b[1])], axis=1 - cb)
    both = contract(jnp.concatenate([a[0], a[1]], axis=ca), jnp.concatenate([above, below], axis=cb), dims)
    half = both.shape[1] // 2
    return both[:, :half] + both[:, half:]


def identity(n):
    rows = lax.broadcasted_iota(jnp.int32, (n, n), 0)
    return (rows == lax.broadcasted_iota(jnp.int32, (n, n), 1)).astype(F32)


def dense_kernel(cols_ref, blocks_ref, order_ref, high_ref, low_ref, columns):
    block_rows, per_row = cols_ref.shape
    blk = blocks_ref.shape[1]
    rows = block_rows * blk
    columns[...] = jnp.zeros_like(columns)
    for q in range(block_rows):
        for n in range(per_row):
            where = (cols_ref[q, n], slice(q * blk, (q + 1) * blk))
            columns[where] = columns[where] + blocks_ref[q * per_row + n]
    tree = jnp.concatenate([columns[c] for c in range(block_rows)], axis=1)
    bead = lax.broadcasted_iota(jnp.int32, (rows, rows), 0)
    select = (bead == order_ref[...]).astype(F32).astype(BF16)
    for piece, out in zip(parts(tree), (high_ref, low_ref)):
        moved = contract(select, piece, ((1,), (0,))).astype(BF16)
        out[...] = contract(moved, select, ((1,), (1,))).astype(BF16)


def panel_kernel(rep_ref, own_ref, *refs):
    reps = len(refs) - 3
    pieces, (high_ref, low_ref, out_ref, basis_scr) = (own_ref, *refs[: reps - 1]), refs[reps - 1:]
    own_levels, narrow, rows = own_ref.shape
    scale = 1.0 / math.sqrt(rows)
    width = reps * narrow
    rep = rep_ref[0]
    for shift, piece in enumerate(pieces):
        source = lax.rem(rep + reps - shift, reps)
        basis_scr[:, pl.ds(pl.multiple_of(source * narrow, narrow), narrow), :] = piece[...]
    panels = []
    for level in range(own_levels):
        basis = parts(basis_scr[level])
        image = product(basis, (high_ref[...], low_ref[...]))
        panels.append(product(parts(image), basis, ((1,), (1,))) * scale)
    pair = parts(panels[0])
    first = product(pair, pair, ((0,), (0,))) * (1.0 / width)
    out_ref[0] = panels[0]
    out_ref[1] = jnp.where(rep == 0, first, panels[1])


def packed(matrix):
    half = matrix.shape[0] // 2
    block = matrix[half:, half:]
    return jnp.concatenate([matrix[:half], jnp.concatenate([block[:half // 2], block[half // 2:]], axis=1)], axis=0)


def unpacked(rows):
    half = rows.shape[1] // 2
    upper, block = rows[:half], rows[half:]
    lower = jnp.concatenate([block[:, :half], block[:, half:]], axis=0)
    return jnp.concatenate([upper, jnp.concatenate([upper[:, half:].T, lower], axis=1)], axis=0)


def level_kernel(first, last, kind, split, side_ref, core_ref, own_ref, pair_ref, *refs):
    width = own_ref.shape[1]
    eye = identity(width)
    side = side_ref[0]
    skip = 1 if first else 0
    if first:
        panel, outs = own_ref[0], refs
    else:
        panel, outs = refs[0][...], refs[1:]

    def theirs(n):
        if kind == "other":
            return pair_ref[n]
        if kind == "pair":
            return pair_ref[1 - side, n]
        if kind == "packed":
            if n:
                return pair_ref[1 - side, width * n - width // 4:width * (n + 1) - width // 4, :]
            return unpacked(pair_ref[1 - side, :width * 3 // 4, :])
        if kind == "halfother":
            return jnp.concatenate([pair_ref[core, n] for core in range(2)], axis=0)
        return jnp.concatenate([pair_ref[core, 1 - side, n] for core in range(2)], axis=0)

    def ours(n):
        return own_ref[n + skip]

    own, other = ours(0), theirs(0)
    total = own + other
    bound = 1.0 + 2.0 * jnp.max(jnp.sum(jnp.abs(total), axis=0))
    if last:
        matrices = [eye + other]
    else:
        matrices = [eye + other, eye + total, eye + 2.0 * total]
        root_half = math.sqrt(0.5)
        next_panel = (ours(1) + theirs(1)) * root_half
    step = 2.0 / (bound + 1.0)
    rho = 1.0 - step
    scale = 2.0 / (2.0 - rho * rho)
    begun = []
    for matrix in matrices:
        residual = eye - step * matrix
        e = parts(residual)
        begun.append(((scale * step) * (eye + residual), (1.0 - scale) * eye + scale * wide_product(e, e)))
    start = (0.5 * scale * rho * rho, tuple(begun))

    def go_on(carry):
        return carry[0] > 1e-2

    def refine(carry):
        rho, inverses = carry
        scale = 2.0 / (2.0 - rho * rho)
        new = []
        for inverse, residual in inverses:
            e = parts(residual)
            better = scale * (inverse + wide_product(parts(inverse), e))
            new.append((better, (1.0 - scale) * eye + scale * wide_product(e, e)))
        return (0.5 * scale * rho * rho, tuple(new))

    _, inverses = lax.while_loop(go_on, refine, start)
    pairs = [parts(matrix) for matrix in matrices]

    def correct(_, found):
        new = []
        for inverse, pair in zip(found, pairs):
            x = parts(inverse)
            new.append(inverse + wide_product(x, parts(eye - wide_product(pair, x))))
        return tuple(new)

    extra = jnp.where(bound > 200.0, 3, 0)
    inverses = lax.fori_loop(0, extra, correct, tuple(inverse for inverse, _ in inverses))
    x = [parts(inverse) for inverse in inverses]
    residuals = [parts(eye - wide_product(pair, inverse)) for pair, inverse in zip(pairs, x)]
    if not last:
        next_panel_ref, next_q_ref, next_ref = outs[1:4]
        p = parts(next_panel)
        r = residuals[2]
        y = wide_product(x[2], p)
        ry, rp = wide_product(r, parts(y)), wide_product(r, p)
        sum_y = next_panel + y
        plain = wide_product(p, parts(sum_y), ((0,), (0,)))
        bent = wide_product(parts(ry), parts(next_panel + rp), ((0,), (0,)))
        next_ref[0] = (plain + bent) * (0.5 / width)
        next_panel_ref[...] = next_panel
        for upper in range(1, next_ref.shape[0]):
            next_ref[upper] = (ours(upper + 1) + theirs(upper + 1)) * root_half
        if split == "packed":
            outs[4][:width * 3 // 4] = packed(next_ref[0])
            for upper in range(1, next_ref.shape[0]):
                outs[4][width * upper - width // 4:width * (upper + 1) - width // 4] = next_ref[upper]
        elif split:
            half_rows = width // 2
            outs[4][...] = next_ref[:, pl.ds(pl.multiple_of(core_ref[0] * half_rows, half_rows), half_rows), :]
        r = residuals[1]
        both = eye - wide_product(pairs[1], x[1]) + wide_product(r, r)
        next_q_ref[...] = 2.0 * eye - (inverses[1] + wide_product(x[1], parts(both)))
    r = residuals[0]
    v = wide_product(parts(panel), x[0])
    vr = wide_product(parts(v), r)
    gained = v + vr + wide_product(parts(vr), r)
    outs[0][...] = jnp.where(side == 1, gained, panel)


def spread(x):
    return jnp.broadcast_to(x, (8, 128))


def reciprocal(x):
    guess = pl.reciprocal(x, approx=True)
    return guess * (2.0 - x * guess)


def eliminate(v, w, k, block, row, sub, area):
    count = len(v)
    area[0] = v[block]
    line = [spread(area[0, row + i:row + i + 1, :]) for i in range(4)]
    line_w = []
    if w:
        area[1] = w[block]
        line_w = [spread(area[1, row + i:row + i + 1, :]) for i in range(4)]
    column = {j: [spread(v[j][:, k + i:k + i + 1]) for i in range(4)] for j in range(block, count)}
    for i in range(4):
        area[2 + i] = column[block][i]
    p = {(i, h): spread(area[2 + i, row + h:row + h + 1, :]) for i in range(4) for h in range(i, 4)}
    inverse = reciprocal(p[0, 0] * p[1, 1] - p[0, 1] * p[0, 1])
    i00, i01, i11 = p[1, 1] * inverse, -(p[0, 1] * inverse), p[0, 0] * inverse
    f02, f12 = i00 * p[0, 2] + i01 * p[1, 2], i01 * p[0, 2] + i11 * p[1, 2]
    f03, f13 = i00 * p[0, 3] + i01 * p[1, 3], i01 * p[0, 3] + i11 * p[1, 3]
    s22 = p[2, 2] - (p[0, 2] * f02 + p[1, 2] * f12)
    s23 = p[2, 3] - (p[0, 2] * f03 + p[1, 2] * f13)
    s33 = p[3, 3] - (p[0, 3] * f03 + p[1, 3] * f13)
    inverse = reciprocal(s22 * s33 - s23 * s23)
    j22, j23, j33 = s33 * inverse, -(s23 * inverse), s22 * inverse
    f01, f23 = p[0, 1] * reciprocal(p[0, 0]), s23 * reciprocal(s22)
    for lines in (line, line_w)[:2 if w else 1]:
        lines[2] = lines[2] - f02 * lines[0] - f12 * lines[1]
        lines[3] = lines[3] - f03 * lines[0] - f13 * lines[1]
    for j in range(block, count):
        c = column[j]
        if j > block or row == 0:
            g0, g1 = i00 * c[0] + i01 * c[1], i01 * c[0] + i11 * c[1]
            e2 = c[2] - c[0] * f02 - c[1] * f12
            e3 = c[3] - c[0] * f03 - c[1] * f13
            g2, g3 = j22 * e2 + j23 * e3, j23 * e2 + j33 * e3
        else:
            g0 = g1 = g2 = g3 = 0.0
        if j == block:
            inside = jnp.where(sub == row + 1, f01, jnp.where(sub == row + 2, f02, jnp.where(sub == row + 3, f03, 0.0)))
            g0 = jnp.where(sub > row + 3, g0, inside)
            g1 = jnp.where(sub > row + 3, g1, jnp.where(sub == row + 2, f12, jnp.where(sub == row + 3, f13, 0.0)))
            g2 = jnp.where(sub > row + 3, g2, jnp.where(sub == row + 3, f23, 0.0))
            g3 = jnp.where(sub > row + 3, g3, 0.0)
        v[j] = v[j] - g0 * line[0] - g1 * line[1] - g2 * line[2] - g3 * line[3]
        if w:
            w[j] = w[j] - g0 * line_w[0] - g1 * line_w[1] - g2 * line_w[2] - g3 * line_w[3]


def whiten_kernel(levels, area, rep_ref, *refs):
    x_refs, p_refs, q_refs = refs[:levels], refs[levels:2 * levels], refs[2 * levels:-1]
    out_ref = refs[-1]
    width = x_refs[0].shape[0]
    narrow = out_ref.shape[1]
    lane = lax.broadcasted_iota(jnp.int32, (8, width), 1)
    sub = lax.broadcasted_iota(jnp.int32, (8, width), 0)
    count = PANEL // 8
    lanes = lax.broadcasted_iota(jnp.int32, (width, width), 1)
    state, columns = [], []
    for m in range(levels):
        x, p = x_refs[m][...], p_refs[m]
        p = p[0] if len(p.shape) == 3 else p[...]
        q = q_refs[m - 1][...] if m else identity(width)
        pair = parts(x)
        state.append(q + product(pair, parts(p), ((1,), (1,))) * (1.0 / width))
        columns.append(pltpu.roll(x, width - rep_ref[0] * narrow, 1))
    done = [[] for _ in range(levels)]
    for top in range(0, width, PANEL):
        left = [[s[8 * j:8 * j + 8] for j in range(count)] for s in state]
        right = [[c[8 * j:8 * j + 8] for j in range(count)] if top == 0 else [] for c in columns]
        for kk in range(0, PANEL, 4):
            for m in range(levels):
                eliminate(left[m], right[m], top + kk, kk // 8, kk % 8, sub, area.at[m, kk // 4 % 2])
        for m in range(levels):
            for j in range(count):
                diagonal = jnp.sum(jnp.where(lane == sub + (top + 8 * j), left[m][j], 0.0), axis=1, keepdims=True)
                root = lax.rsqrt(diagonal)
                left[m][j] = left[m][j] * root
                if top == 0:
                    right[m][j] = right[m][j] * root
            upper = jnp.concatenate(left[m], axis=0)
            both = upper
            if top == 0:
                both = jnp.where(lanes[:PANEL] < narrow, jnp.concatenate(right[m], axis=0), upper)
            done[m].append(both)
            if top + PANEL < width:
                rest = state[m][PANEL:]
                if top == 0:
                    rest = jnp.where(lanes[PANEL:] < narrow, columns[m][PANEL:], rest)
                state[m] = rest - product(parts(upper.T[top + PANEL:]), parts(both))
    for m in range(levels):
        out_ref[m] = jnp.concatenate(done[m], axis=0).T[:narrow]


def last_kernel(levels, kind, side_ref, core_ref, rep_ref, own_ref, pair_ref, *refs):
    x_refs, p_refs, q_refs = refs[: levels - 1], refs[levels - 1:2 * levels - 1], refs[2 * levels - 1:-3]
    out_ref, x_last, area = refs[-3:]
    level_kernel(False, True, kind, False, side_ref, core_ref, own_ref, pair_ref, p_refs[-1], x_last)
    whiten_kernel(levels, area, rep_ref, *x_refs, x_last, *p_refs, *q_refs, out_ref)


def call(kernel, out_shape, n_smem, n_vmem, scratch=()):
    return pl.pallas_call(
        kernel,
        out_shape=out_shape,
        in_specs=[pl.BlockSpec(memory_space=pltpu.SMEM)] * n_smem
        + [pl.BlockSpec(memory_space=pltpu.VMEM)] * n_vmem,
        out_specs=jax.tree.map(lambda _: pl.BlockSpec(memory_space=pltpu.VMEM), out_shape),
        scratch_shapes=list(scratch),
        compiler_params=pltpu.CompilerParams(vmem_limit_bytes=VMEM_BYTES),
    )


def partner(leaf, bit):
    if bit == 0:
        return leaf ^ 1
    if bit == 1:
        return leaf ^ 2
    if bit == 2:
        return leaf ^ 6
    if bit == 4:
        return leaf ^ 24
    if bit == 6:
        z = leaf >> 3
        z = (z + 4) % 16 if z & 4 else (z - 4) % 16
        return z * 8 + (leaf & 7)
    return leaf ^ (1 << bit)


def pair_gathered(value, axis, bit):
    leaves = range(lax.axis_size(axis))
    groups = [[leaf, partner(leaf, bit)] for leaf in leaves if not leaf >> bit & 1]
    return lax.all_gather(value, axis, axis=0, axis_index_groups=groups)


def swapped(value, axis, bit):
    pairs = [(source, partner(source, bit)) for source in range(lax.axis_size(axis))]
    return lax.ppermute(value, axis, pairs)


def local(basis, near_blocks, near_cols, bead_order):
    levels, narrow, rows = basis.shape
    block_rows, per_row = near_cols.shape
    blk = rows // block_rows
    reps = lax.axis_size("rep")
    width = reps * narrow
    leaf_index = lax.axis_index("leaf")
    rep_index = lax.axis_index("rep")
    rep_scalar = rep_index.astype(jnp.int32).reshape(1)
    square = jax.ShapeDtypeStruct((width, width), F32)

    def levels_of(rep):
        return lax.dynamic_slice_in_dim(basis, jnp.maximum(2 * rep - 1, 0), 2, 0)

    pieces = [levels_of(rep_index)]
    for shift in range(1, reps):
        pairs = [(source, (source + shift) % reps) for source in range(reps)]
        pieces.append(lax.ppermute(levels_of(lax.rem(rep_index + shift, reps)), "rep", pairs))
    tiles = near_blocks.reshape(block_rows * per_row, blk, blk)
    dense = [jax.ShapeDtypeStruct((rows, rows), BF16)] * 2
    high, low = call(dense_kernel, dense, 1, 2, [pltpu.VMEM((block_rows, rows, blk), F32)])(
        near_cols, tiles, bead_order
    )
    two = jax.ShapeDtypeStruct((2, width, width), F32)
    mine = call(panel_kernel, two, 1, reps + 2, [pltpu.VMEM((2, width, rows), F32)])(
        rep_scalar, *pieces, high, low
    )
    sent = lax.all_gather(mine, "rep", axis=0, tiled=True)
    core = (leaf_index & 1).astype(jnp.int32).reshape(1)
    half = panel = None
    x_list, p_list, q_list = [], [sent], []
    for bit in range(levels):
        first, last = bit == 0, bit == levels - 1
        kind = EXCHANGE[bit]
        value = half if kind[0] in "hp" and half is not None else sent[1:] if first else sent
        pair = (swapped if kind.endswith("other") else pair_gathered)(value, "leaf", bit)
        if kind.startswith("half"):
            pair = pair_gathered(pair, "leaf", 0)
        side = (leaf_index >> bit & 1).astype(jnp.int32).reshape(1)
        split = "" if last or EXCHANGE[bit + 1] in ("pair", "other") else EXCHANGE[bit + 1]
        shapes = [square]
        if not last:
            count = levels - bit - 1
            shapes += [square, square, jax.ShapeDtypeStruct((count, width, width), F32)]
            if split == "packed":
                shapes.append(jax.ShapeDtypeStruct((count * width - width // 4, width), F32))
            elif split:
                shapes.append(jax.ShapeDtypeStruct((count, width // 2, width), F32))
        kernel = functools.partial(level_kernel, first, last, kind, split)
        state = [] if first else [panel]
        if last:
            out = jax.ShapeDtypeStruct((levels, narrow, width), F32)
            kernel = functools.partial(last_kernel, levels, kind)
            scratch = [pltpu.VMEM((width, width), F32), pltpu.VMEM((levels, 2, 6, 8, width), F32)]
            return call(kernel, out, 3, 3 * levels, scratch)(
                side, core, rep_scalar, sent, pair, *x_list, *p_list, *q_list
            )
        x, panel, q, sent, *rest = call(kernel, shapes, 2, 2 + len(state))(side, core, sent, pair, *state)
        half = rest[0] if rest else None
        x_list.append(x)
        p_list.append(panel)
        q_list.append(q)


def solution(mesh):
    return jax.shard_map(
        local,
        mesh=mesh,
        in_specs=(P(None, "rep", "leaf"), P("leaf", None, None), P("leaf", None), P("leaf", None)),
        out_specs=P(None, "rep", "leaf"),
        check_vma=False,
    )
```

```python
import functools
import math

import jax
import jax.numpy as jnp
from jax import lax
from jax.experimental import pallas as pl
from jax.experimental.pallas import tpu as pltpu
from jax.sharding import PartitionSpec as P

F32 = jnp.float32
BF16 = jnp.bfloat16
PANEL = 32
EXCHANGE = ("pair",) * 5 + ("packed", "packed")
VMEM_BYTES = 48 * 1024 * 1024


def parts(x):
    high = x.astype(BF16)
    return high, (x - high.astype(F32)).astype(BF16)


def contract(a, b, dims):
    return lax.dot_general(a, b, (dims, ((), ())), preferred_element_type=F32)


def product(a, b, dims=((1,), (0,))):
    return contract(a[0], b[0], dims) + (contract(a[0], b[1], dims) + contract(a[1], b[0], dims))


def wide_product(a, b, dims=((1,), (0,))):
    (ca,), (cb,) = dims
    above = jnp.concatenate([b[0], b[1]], axis=1 - cb)
    below = jnp.concatenate([b[0], jnp.zeros_like(b[1])], axis=1 - cb)
    both = contract(jnp.concatenate([a[0], a[1]], axis=ca), jnp.concatenate([above, below], axis=cb), dims)
    half = both.shape[1] // 2
    return both[:, :half] + both[:, half:]


def identity(n):
    rows = lax.broadcasted_iota(jnp.int32, (n, n), 0)
    return (rows == lax.broadcasted_iota(jnp.int32, (n, n), 1)).astype(F32)


def dense_kernel(cols_ref, blocks_ref, order_ref, high_ref, low_ref, columns):
    block_rows, per_row = cols_ref.shape
    blk = blocks_ref.shape[1]
    rows = block_rows * blk
    columns[...] = jnp.zeros_like(columns)
    for q in range(block_rows):
        for n in range(per_row):
            where = (cols_ref[q, n], slice(q * blk, (q + 1) * blk))
            columns[where] = columns[where] + blocks_ref[q * per_row + n]
    tree = jnp.concatenate([columns[c] for c in range(block_rows)], axis=1)
    bead = lax.broadcasted_iota(jnp.int32, (rows, rows), 0)
    select = (bead == order_ref[...]).astype(F32).astype(BF16)
    for piece, out in zip(parts(tree), (high_ref, low_ref)):
        moved = contract(select, piece, ((1,), (0,))).astype(BF16)
        out[...] = contract(moved, select, ((1,), (1,))).astype(BF16)


def panel_kernel(rep_ref, own_ref, *refs):
    reps = len(refs) - 3
    pieces, (high_ref, low_ref, out_ref, basis_scr) = (own_ref, *refs[: reps - 1]), refs[reps - 1:]
    own_levels, narrow, rows = own_ref.shape
    scale = 1.0 / math.sqrt(rows)
    width = reps * narrow
    rep = rep_ref[0]
    for shift, piece in enumerate(pieces):
        source = lax.rem(rep + reps - shift, reps)
        basis_scr[:, pl.ds(pl.multiple_of(source * narrow, narrow), narrow), :] = piece[...]
    panels = []
    for level in range(own_levels):
        basis = parts(basis_scr[level])
        image = product(basis, (high_ref[...], low_ref[...]))
        panels.append(product(parts(image), basis, ((1,), (1,))) * scale)
    pair = parts(panels[0])
    first = product(pair, pair, ((0,), (0,))) * (1.0 / width)
    out_ref[0] = panels[0]
    out_ref[1] = jnp.where(rep == 0, first, panels[1])


def packed(matrix):
    half = matrix.shape[0] // 2
    block = matrix[half:, half:]
    return jnp.concatenate([matrix[:half], jnp.concatenate([block[:half // 2], block[half // 2:]], axis=1)], axis=0)


def unpacked(rows):
    half = rows.shape[1] // 2
    upper, block = rows[:half], rows[half:]
    lower = jnp.concatenate([block[:, :half], block[:, half:]], axis=0)
    return jnp.concatenate([upper, jnp.concatenate([upper[:, half:].T, lower], axis=1)], axis=0)


def level_kernel(first, last, kind, split, side_ref, core_ref, own_ref, pair_ref, *refs):
    width = own_ref.shape[1]
    eye = identity(width)
    side = side_ref[0]
    skip = 1 if first else 0
    if first:
        panel, outs = own_ref[0], refs
    else:
        panel, outs = refs[0][...], refs[1:]

    def theirs(n):
        if kind == "other":
            return pair_ref[n]
        if kind == "pair":
            return pair_ref[1 - side, n]
        if kind == "packed":
            if n:
                return pair_ref[1 - side, width * n - width // 4:width * (n + 1) - width // 4, :]
            return unpacked(pair_ref[1 - side, :width * 3 // 4, :])
        if kind == "halfother":
            return jnp.concatenate([pair_ref[core, n] for core in range(2)], axis=0)
        return jnp.concatenate([pair_ref[core, 1 - side, n] for core in range(2)], axis=0)

    def ours(n):
        return own_ref[n + skip]

    own, other = ours(0), theirs(0)
    total = own + other
    bound = 1.0 + 2.0 * jnp.max(jnp.sum(jnp.abs(total), axis=0))
    if last:
        matrices = [eye + other]
    else:
        matrices = [eye + other, eye + total, eye + 2.0 * total]
        root_half = math.sqrt(0.5)
        next_panel = (ours(1) + theirs(1)) * root_half
    step = 2.0 / (bound + 1.0)
    rho = 1.0 - step
    scale = 2.0 / (2.0 - rho * rho)
    begun = []
    for matrix in matrices:
        residual = eye - step * matrix
        e = parts(residual)
        begun.append(((scale * step) * (eye + residual), (1.0 - scale) * eye + scale * wide_product(e, e)))
    start = (0.5 * scale * rho * rho, tuple(begun))

    def go_on(carry):
        return carry[0] > 1e-2

    def refine(carry):
        rho, inverses = carry
        scale = 2.0 / (2.0 - rho * rho)
        new = []
        for inverse, residual in inverses:
            e = parts(residual)
            better = scale * (inverse + wide_product(parts(inverse), e))
            new.append((better, (1.0 - scale) * eye + scale * wide_product(e, e)))
        return (0.5 * scale * rho * rho, tuple(new))

    _, inverses = lax.while_loop(go_on, refine, start)
    pairs = [parts(matrix) for matrix in matrices]

    def correct(_, found):
        new = []
        for inverse, pair in zip(found, pairs):
            x = parts(inverse)
            new.append(inverse + wide_product(x, parts(eye - wide_product(pair, x))))
        return tuple(new)

    extra = jnp.where(bound > 200.0, 3, 0)
    inverses = lax.fori_loop(0, extra, correct, tuple(inverse for inverse, _ in inverses))
    x = [parts(inverse) for inverse in inverses]
    residuals = [parts(eye - wide_product(pair, inverse)) for pair, inverse in zip(pairs, x)]
    if not last:
        next_panel_ref, next_q_ref, next_ref = outs[1:4]
        p = parts(next_panel)
        r = residuals[2]
        y = wide_product(x[2], p)
        ry, rp = wide_product(r, parts(y)), wide_product(r, p)
        sum_y = next_panel + y
        plain = wide_product(p, parts(sum_y), ((0,), (0,)))
        bent = wide_product(parts(ry), parts(next_panel + rp), ((0,), (0,)))
        next_ref[0] = (plain + bent) * (0.5 / width)
        next_panel_ref[...] = next_panel
        for upper in range(1, next_ref.shape[0]):
            next_ref[upper] = (ours(upper + 1) + theirs(upper + 1)) * root_half
        if split == "packed":
            outs[4][:width * 3 // 4] = packed(next_ref[0])
            for upper in range(1, next_ref.shape[0]):
                outs[4][width * upper - width // 4:width * (upper + 1) - width // 4] = next_ref[upper]
        elif split:
            half_rows = width // 2
            outs[4][...] = next_ref[:, pl.ds(pl.multiple_of(core_ref[0] * half_rows, half_rows), half_rows), :]
        r = residuals[1]
        both = eye - wide_product(pairs[1], x[1]) + wide_product(r, r)
        next_q_ref[...] = 2.0 * eye - (inverses[1] + wide_product(x[1], parts(both)))
    r = residuals[0]
    v = wide_product(parts(panel), x[0])
    vr = wide_product(parts(v), r)
    gained = v + vr + wide_product(parts(vr), r)
    outs[0][...] = jnp.where(side == 1, gained, panel)


def spread(x):
    return jnp.broadcast_to(x, (8, 128))


def reciprocal(x):
    guess = pl.reciprocal(x, approx=True)
    return guess * (2.0 - x * guess)


def eliminate(v, w, k, block, row, sub, area):
    count = len(v)
    area[0] = v[block]
    line = [spread(area[0, row + i:row + i + 1, :]) for i in range(4)]
    line_w = []
    if w:
        area[1] = w[block]
        line_w = [spread(area[1, row + i:row + i + 1, :]) for i in range(4)]
    column = {j: [spread(v[j][:, k + i:k + i + 1]) for i in range(4)] for j in range(block, count)}
    for i in range(4):
        area[2 + i] = column[block][i]
    p = {(i, h): spread(area[2 + i, row + h:row + h + 1, :]) for i in range(4) for h in range(i, 4)}
    inverse = reciprocal(p[0, 0] * p[1, 1] - p[0, 1] * p[0, 1])
    i00, i01, i11 = p[1, 1] * inverse, -(p[0, 1] * inverse), p[0, 0] * inverse
    f02, f12 = i00 * p[0, 2] + i01 * p[1, 2], i01 * p[0, 2] + i11 * p[1, 2]
    f03, f13 = i00 * p[0, 3] + i01 * p[1, 3], i01 * p[0, 3] + i11 * p[1, 3]
    s22 = p[2, 2] - (p[0, 2] * f02 + p[1, 2] * f12)
    s23 = p[2, 3] - (p[0, 2] * f03 + p[1, 2] * f13)
    s33 = p[3, 3] - (p[0, 3] * f03 + p[1, 3] * f13)
    inverse = reciprocal(s22 * s33 - s23 * s23)
    j22, j23, j33 = s33 * inverse, -(s23 * inverse), s22 * inverse
    f01, f23 = p[0, 1] * reciprocal(p[0, 0]), s23 * reciprocal(s22)
    for lines in (line, line_w)[:2 if w else 1]:
        lines[2] = lines[2] - f02 * lines[0] - f12 * lines[1]
        lines[3] = lines[3] - f03 * lines[0] - f13 * lines[1]
    for j in range(block, count):
        c = column[j]
        if j > block or row == 0:
            g0, g1 = i00 * c[0] + i01 * c[1], i01 * c[0] + i11 * c[1]
            e2 = c[2] - c[0] * f02 - c[1] * f12
            e3 = c[3] - c[0] * f03 - c[1] * f13
            g2, g3 = j22 * e2 + j23 * e3, j23 * e2 + j33 * e3
        else:
            g0 = g1 = g2 = g3 = 0.0
        if j == block:
            inside = jnp.where(sub == row + 1, f01, jnp.where(sub == row + 2, f02, jnp.where(sub == row + 3, f03, 0.0)))
            g0 = jnp.where(sub > row + 3, g0, inside)
            g1 = jnp.where(sub > row + 3, g1, jnp.where(sub == row + 2, f12, jnp.where(sub == row + 3, f13, 0.0)))
            g2 = jnp.where(sub > row + 3, g2, jnp.where(sub == row + 3, f23, 0.0))
            g3 = jnp.where(sub > row + 3, g3, 0.0)
        v[j] = v[j] - g0 * line[0] - g1 * line[1] - g2 * line[2] - g3 * line[3]
        if w:
            w[j] = w[j] - g0 * line_w[0] - g1 * line_w[1] - g2 * line_w[2] - g3 * line_w[3]


def whiten_kernel(levels, area, rep_ref, *refs):
    x_refs, p_refs, q_refs = refs[:levels], refs[levels:2 * levels], refs[2 * levels:-1]
    out_ref = refs[-1]
    width = x_refs[0].shape[0]
    narrow = out_ref.shape[1]
    lane = lax.broadcasted_iota(jnp.int32, (8, width), 1)
    sub = lax.broadcasted_iota(jnp.int32, (8, width), 0)
    count = PANEL // 8
    lanes = lax.broadcasted_iota(jnp.int32, (width, width), 1)
    state, columns = [], []
    for m in range(levels):
        x, p = x_refs[m][...], p_refs[m]
        p = p[0] if len(p.shape) == 3 else p[...]
        q = q_refs[m - 1][...] if m else identity(width)
        pair = parts(x)
        state.append(q + product(pair, parts(p), ((1,), (1,))) * (1.0 / width))
        columns.append(pltpu.roll(x, width - rep_ref[0] * narrow, 1))
    done = [[] for _ in range(levels)]
    for top in range(0, width, PANEL):
        left = [[s[8 * j:8 * j + 8] for j in range(count)] for s in state]
        right = [[c[8 * j:8 * j + 8] for j in range(count)] if top == 0 else [] for c in columns]
        for kk in range(0, PANEL, 4):
            for m in range(levels):
                eliminate(left[m], right[m], top + kk, kk // 8, kk % 8, sub, area.at[m, kk // 4 % 2])
        for m in range(levels):
            for j in range(count):
                diagonal = jnp.sum(jnp.where(lane == sub + (top + 8 * j), left[m][j], 0.0), axis=1, keepdims=True)
                root = lax.rsqrt(diagonal)
                left[m][j] = left[m][j] * root
                if top == 0:
                    right[m][j] = right[m][j] * root
            upper = jnp.concatenate(left[m], axis=0)
            both = upper
            if top == 0:
                both = jnp.where(lanes[:PANEL] < narrow, jnp.concatenate(right[m], axis=0), upper)
            done[m].append(both)
            if top + PANEL < width:
                rest = state[m][PANEL:]
                if top == 0:
                    rest = jnp.where(lanes[PANEL:] < narrow, columns[m][PANEL:], rest)
                state[m] = rest - product(parts(upper.T[top + PANEL:]), parts(both))
    for m in range(levels):
        out_ref[m] = jnp.concatenate(done[m], axis=0).T[:narrow]


def last_kernel(levels, kind, side_ref, core_ref, rep_ref, own_ref, pair_ref, *refs):
    x_refs, p_refs, q_refs = refs[: levels - 1], refs[levels - 1:2 * levels - 1], refs[2 * levels - 1:-3]
    out_ref, x_last, area = refs[-3:]
    level_kernel(False, True, kind, False, side_ref, core_ref, own_ref, pair_ref, p_refs[-1], x_last)
    whiten_kernel(levels, area, rep_ref, *x_refs, x_last, *p_refs, *q_refs, out_ref)


def call(kernel, out_shape, n_smem, n_vmem, scratch=()):
    return pl.pallas_call(
        kernel,
        out_shape=out_shape,
        in_specs=[pl.BlockSpec(memory_space=pltpu.SMEM)] * n_smem
        + [pl.BlockSpec(memory_space=pltpu.VMEM)] * n_vmem,
        out_specs=jax.tree.map(lambda _: pl.BlockSpec(memory_space=pltpu.VMEM), out_shape),
        scratch_shapes=list(scratch),
        compiler_params=pltpu.CompilerParams(vmem_limit_bytes=VMEM_BYTES),
    )


def partner(leaf, bit):
    if bit == 0:
        return leaf ^ 1
    if bit == 1:
        return leaf ^ 2
    if bit == 2:
        return leaf ^ 6
    if bit == 4:
        return leaf ^ 24
    if bit == 5:
        return leaf ^ 56
    if bit == 6:
        z = leaf >> 3
        z = (z + 4) % 16 if z & 4 else (z - 4) % 16
        return z * 8 + (leaf & 7)
    return leaf ^ (1 << bit)


def pair_gathered(value, axis, bit):
    leaves = range(lax.axis_size(axis))
    groups = [[leaf, partner(leaf, bit)] for leaf in leaves if not leaf >> bit & 1]
    return lax.all_gather(value, axis, axis=0, axis_index_groups=groups)


def swapped(value, axis, bit):
    pairs = [(source, partner(source, bit)) for source in range(lax.axis_size(axis))]
    return lax.ppermute(value, axis, pairs)


def local(basis, near_blocks, near_cols, bead_order):
    levels, narrow, rows = basis.shape
    block_rows, per_row = near_cols.shape
    blk = rows // block_rows
    reps = lax.axis_size("rep")
    width = reps * narrow
    leaf_index = lax.axis_index("leaf")
    rep_index = lax.axis_index("rep")
    rep_scalar = rep_index.astype(jnp.int32).reshape(1)
    square = jax.ShapeDtypeStruct((width, width), F32)

    def levels_of(rep):
        return lax.dynamic_slice_in_dim(basis, jnp.maximum(2 * rep - 1, 0), 2, 0)

    pieces = [levels_of(rep_index)]
    for shift in range(1, reps):
        pairs = [(source, (source + shift) % reps) for source in range(reps)]
        pieces.append(lax.ppermute(levels_of(lax.rem(rep_index + shift, reps)), "rep", pairs))
    tiles = near_blocks.reshape(block_rows * per_row, blk, blk)
    dense = [jax.ShapeDtypeStruct((rows, rows), BF16)] * 2
    high, low = call(dense_kernel, dense, 1, 2, [pltpu.VMEM((block_rows, rows, blk), F32)])(
        near_cols, tiles, bead_order
    )
    two = jax.ShapeDtypeStruct((2, width, width), F32)
    mine = call(panel_kernel, two, 1, reps + 2, [pltpu.VMEM((2, width, rows), F32)])(
        rep_scalar, *pieces, high, low
    )
    sent = lax.all_gather(mine, "rep", axis=0, tiled=True)
    core = (leaf_index & 1).astype(jnp.int32).reshape(1)
    half = panel = None
    x_list, p_list, q_list = [], [sent], []
    for bit in range(levels):
        first, last = bit == 0, bit == levels - 1
        kind = EXCHANGE[bit]
        value = half if kind[0] in "hp" and half is not None else sent[1:] if first else sent
        pair = (swapped if kind.endswith("other") else pair_gathered)(value, "leaf", bit)
        if kind.startswith("half"):
            pair = pair_gathered(pair, "leaf", 0)
        side = (leaf_index >> bit & 1).astype(jnp.int32).reshape(1)
        split = "" if last or EXCHANGE[bit + 1] in ("pair", "other") else EXCHANGE[bit + 1]
        shapes = [square]
        if not last:
            count = levels - bit - 1
            shapes += [square, square, jax.ShapeDtypeStruct((count, width, width), F32)]
            if split == "packed":
                shapes.append(jax.ShapeDtypeStruct((count * width - width // 4, width), F32))
            elif split:
                shapes.append(jax.ShapeDtypeStruct((count, width // 2, width), F32))
        kernel = functools.partial(level_kernel, first, last, kind, split)
        state = [] if first else [panel]
        if last:
            out = jax.ShapeDtypeStruct((levels, narrow, width), F32)
            kernel = functools.partial(last_kernel, levels, kind)
            scratch = [pltpu.VMEM((width, width), F32), pltpu.VMEM((levels, 2, 6, 8, width), F32)]
            return call(kernel, out, 3, 3 * levels, scratch)(
                side, core, rep_scalar, sent, pair, *x_list, *p_list, *q_list
            )
        x, panel, q, sent, *rest = call(kernel, shapes, 2, 2 + len(state))(side, core, sent, pair, *state)
        half = rest[0] if rest else None
        x_list.append(x)
        p_list.append(panel)
        q_list.append(q)


def solution(mesh):
    return jax.shard_map(
        local,
        mesh=mesh,
        in_specs=(P(None, "rep", "leaf"), P("leaf", None, None), P("leaf", None), P("leaf", None)),
        out_specs=P(None, "rep", "leaf"),
        check_vma=False,
    )
```

```python
import functools
import math

import jax
import jax.numpy as jnp
from jax import lax
from jax.experimental import pallas as pl
from jax.experimental.pallas import tpu as pltpu
from jax.sharding import PartitionSpec as P

F32 = jnp.float32
BF16 = jnp.bfloat16
PANEL = 32
EXCHANGE = ("pair",) * 5 + ("packed", "packed")
VMEM_BYTES = 48 * 1024 * 1024


def parts(x):
    high = x.astype(BF16)
    return high, (x - high.astype(F32)).astype(BF16)


def contract(a, b, dims):
    return lax.dot_general(a, b, (dims, ((), ())), preferred_element_type=F32)


def product(a, b, dims=((1,), (0,))):
    return contract(a[0], b[0], dims) + (contract(a[0], b[1], dims) + contract(a[1], b[0], dims))


def wide_product(a, b, dims=((1,), (0,))):
    (ca,), (cb,) = dims
    above = jnp.concatenate([b[0], b[1]], axis=1 - cb)
    below = jnp.concatenate([b[0], jnp.zeros_like(b[1])], axis=1 - cb)
    both = contract(jnp.concatenate([a[0], a[1]], axis=ca), jnp.concatenate([above, below], axis=cb), dims)
    half = both.shape[1] // 2
    return both[:, :half] + both[:, half:]


def identity(n):
    rows = lax.broadcasted_iota(jnp.int32, (n, n), 0)
    return (rows == lax.broadcasted_iota(jnp.int32, (n, n), 1)).astype(F32)


def dense_kernel(cols_ref, blocks_ref, order_ref, high_ref, low_ref, columns):
    block_rows, per_row = cols_ref.shape
    blk = blocks_ref.shape[1]
    rows = block_rows * blk
    columns[...] = jnp.zeros_like(columns)
    for q in range(block_rows):
        for n in range(per_row):
            where = (cols_ref[q, n], slice(q * blk, (q + 1) * blk))
            columns[where] = columns[where] + blocks_ref[q * per_row + n]
    tree = jnp.concatenate([columns[c] for c in range(block_rows)], axis=1)
    bead = lax.broadcasted_iota(jnp.int32, (rows, rows), 0)
    select = (bead == order_ref[...]).astype(F32).astype(BF16)
    for piece, out in zip(parts(tree), (high_ref, low_ref)):
        moved = contract(select, piece, ((1,), (0,))).astype(BF16)
        out[...] = contract(moved, select, ((1,), (1,))).astype(BF16)


def panel_kernel(rep_ref, own_ref, *refs):
    reps = len(refs) - 3
    pieces, (high_ref, low_ref, out_ref, basis_scr) = (own_ref, *refs[: reps - 1]), refs[reps - 1:]
    own_levels, narrow, rows = own_ref.shape
    scale = 1.0 / math.sqrt(rows)
    width = reps * narrow
    rep = rep_ref[0]
    for shift, piece in enumerate(pieces):
        source = lax.rem(rep + reps - shift, reps)
        basis_scr[:, pl.ds(pl.multiple_of(source * narrow, narrow), narrow), :] = piece[...]
    panels = []
    for level in range(own_levels):
        basis = parts(basis_scr[level])
        image = product(basis, (high_ref[...], low_ref[...]))
        panels.append(product(parts(image), basis, ((1,), (1,))) * scale)
    pair = parts(panels[0])
    first = product(pair, pair, ((0,), (0,))) * (1.0 / width)
    out_ref[0] = panels[0]
    out_ref[1] = jnp.where(rep == 0, first, panels[1])


def packed(matrix):
    half = matrix.shape[0] // 2
    block = matrix[half:, half:]
    return jnp.concatenate([matrix[:half], jnp.concatenate([block[:half // 2], block[half // 2:]], axis=1)], axis=0)


def unpacked(rows):
    half = rows.shape[1] // 2
    upper, block = rows[:half], rows[half:]
    lower = jnp.concatenate([block[:, :half], block[:, half:]], axis=0)
    return jnp.concatenate([upper, jnp.concatenate([upper[:, half:].T, lower], axis=1)], axis=0)


def level_kernel(first, last, kind, split, side_ref, core_ref, own_ref, pair_ref, *refs):
    width = own_ref.shape[1]
    eye = identity(width)
    side = side_ref[0]
    skip = 1 if first else 0
    if first:
        panel, outs = own_ref[0], refs
    else:
        panel, outs = refs[0][...], refs[1:]

    def theirs(n):
        if kind == "other":
            return pair_ref[n]
        if kind == "pair":
            return pair_ref[1 - side, n]
        if kind == "packed":
            if n:
                return pair_ref[1 - side, width * n - width // 4:width * (n + 1) - width // 4, :]
            return unpacked(pair_ref[1 - side, :width * 3 // 4, :])
        if kind == "halfother":
            return jnp.concatenate([pair_ref[core, n] for core in range(2)], axis=0)
        return jnp.concatenate([pair_ref[core, 1 - side, n] for core in range(2)], axis=0)

    def ours(n):
        return own_ref[n + skip]

    own, other = ours(0), theirs(0)
    total = own + other
    bound = 1.0 + 2.0 * jnp.max(jnp.sum(jnp.abs(total), axis=0))
    if last:
        matrices = [eye + other]
    else:
        matrices = [eye + other, eye + total, eye + 2.0 * total]
        root_half = math.sqrt(0.5)
        next_panel = (ours(1) + theirs(1)) * root_half
    step = 2.0 / (bound + 1.0)
    rho = 1.0 - step
    scale = 2.0 / (2.0 - rho * rho)
    begun = []
    for matrix in matrices:
        residual = eye - step * matrix
        e = parts(residual)
        begun.append(((scale * step) * (eye + residual), (1.0 - scale) * eye + scale * wide_product(e, e)))
    start = (0.5 * scale * rho * rho, tuple(begun))

    def go_on(carry):
        return carry[0] > 1e-2

    def refine(carry):
        rho, inverses = carry
        scale = 2.0 / (2.0 - rho * rho)
        new = []
        for inverse, residual in inverses:
            e = parts(residual)
            better = scale * (inverse + wide_product(parts(inverse), e))
            new.append((better, (1.0 - scale) * eye + scale * wide_product(e, e)))
        return (0.5 * scale * rho * rho, tuple(new))

    _, inverses = lax.while_loop(go_on, refine, start)
    pairs = [parts(matrix) for matrix in matrices]

    def correct(_, found):
        new = []
        for inverse, pair in zip(found, pairs):
            x = parts(inverse)
            new.append(inverse + wide_product(x, parts(eye - wide_product(pair, x))))
        return tuple(new)

    extra = jnp.where(bound > 200.0, 3, 0)
    inverses = lax.fori_loop(0, extra, correct, tuple(inverse for inverse, _ in inverses))
    x = [parts(inverse) for inverse in inverses]
    residuals = [parts(eye - wide_product(pair, inverse)) for pair, inverse in zip(pairs, x)]
    if not last:
        next_panel_ref, next_q_ref, next_ref = outs[1:4]
        p = parts(next_panel)
        r = residuals[2]
        y = wide_product(x[2], p)
        ry, rp = wide_product(r, parts(y)), wide_product(r, p)
        sum_y = next_panel + y
        plain = wide_product(p, parts(sum_y), ((0,), (0,)))
        bent = wide_product(parts(ry), parts(next_panel + rp), ((0,), (0,)))
        next_ref[0] = (plain + bent) * (0.5 / width)
        next_panel_ref[...] = next_panel
        for upper in range(1, next_ref.shape[0]):
            next_ref[upper] = (ours(upper + 1) + theirs(upper + 1)) * root_half
        if split == "packed":
            outs[4][:width * 3 // 4] = packed(next_ref[0])
            for upper in range(1, next_ref.shape[0]):
                outs[4][width * upper - width // 4:width * (upper + 1) - width // 4] = next_ref[upper]
        elif split:
            half_rows = width // 2
            outs[4][...] = next_ref[:, pl.ds(pl.multiple_of(core_ref[0] * half_rows, half_rows), half_rows), :]
        r = residuals[1]
        both = eye - wide_product(pairs[1], x[1]) + wide_product(r, r)
        next_q_ref[...] = 2.0 * eye - (inverses[1] + wide_product(x[1], parts(both)))
    r = residuals[0]
    v = wide_product(parts(panel), x[0])
    vr = wide_product(parts(v), r)
    gained = v + vr + wide_product(parts(vr), r)
    outs[0][...] = jnp.where(side == 1, gained, panel)


def spread(x):
    return jnp.broadcast_to(x, (8, 128))


def reciprocal(x):
    guess = pl.reciprocal(x, approx=True)
    return guess * (2.0 - x * guess)


def eliminate(v, w, k, block, row, sub, area):
    count = len(v)
    area[0] = v[block]
    line = [spread(area[0, row + i:row + i + 1, :]) for i in range(4)]
    line_w = []
    if w:
        area[1] = w[block]
        line_w = [spread(area[1, row + i:row + i + 1, :]) for i in range(4)]
    column = {j: [spread(v[j][:, k + i:k + i + 1]) for i in range(4)] for j in range(block, count)}
    for i in range(4):
        area[2 + i] = column[block][i]
    p = {(i, h): spread(area[2 + i, row + h:row + h + 1, :]) for i in range(4) for h in range(i, 4)}
    inverse = reciprocal(p[0, 0] * p[1, 1] - p[0, 1] * p[0, 1])
    i00, i01, i11 = p[1, 1] * inverse, -(p[0, 1] * inverse), p[0, 0] * inverse
    f02, f12 = i00 * p[0, 2] + i01 * p[1, 2], i01 * p[0, 2] + i11 * p[1, 2]
    f03, f13 = i00 * p[0, 3] + i01 * p[1, 3], i01 * p[0, 3] + i11 * p[1, 3]
    s22 = p[2, 2] - (p[0, 2] * f02 + p[1, 2] * f12)
    s23 = p[2, 3] - (p[0, 2] * f03 + p[1, 2] * f13)
    s33 = p[3, 3] - (p[0, 3] * f03 + p[1, 3] * f13)
    inverse = reciprocal(s22 * s33 - s23 * s23)
    j22, j23, j33 = s33 * inverse, -(s23 * inverse), s22 * inverse
    f01, f23 = p[0, 1] * reciprocal(p[0, 0]), s23 * reciprocal(s22)
    for lines in (line, line_w)[:2 if w else 1]:
        lines[2] = lines[2] - f02 * lines[0] - f12 * lines[1]
        lines[3] = lines[3] - f03 * lines[0] - f13 * lines[1]
    for j in range(block, count):
        c = column[j]
        if j > block or row == 0:
            g0, g1 = i00 * c[0] + i01 * c[1], i01 * c[0] + i11 * c[1]
            e2 = c[2] - c[0] * f02 - c[1] * f12
            e3 = c[3] - c[0] * f03 - c[1] * f13
            g2, g3 = j22 * e2 + j23 * e3, j23 * e2 + j33 * e3
        else:
            g0 = g1 = g2 = g3 = 0.0
        if j == block:
            inside = jnp.where(sub == row + 1, f01, jnp.where(sub == row + 2, f02, jnp.where(sub == row + 3, f03, 0.0)))
            g0 = jnp.where(sub > row + 3, g0, inside)
            g1 = jnp.where(sub > row + 3, g1, jnp.where(sub == row + 2, f12, jnp.where(sub == row + 3, f13, 0.0)))
            g2 = jnp.where(sub > row + 3, g2, jnp.where(sub == row + 3, f23, 0.0))
            g3 = jnp.where(sub > row + 3, g3, 0.0)
        v[j] = v[j] - g0 * line[0] - g1 * line[1] - g2 * line[2] - g3 * line[3]
        if w:
            w[j] = w[j] - g0 * line_w[0] - g1 * line_w[1] - g2 * line_w[2] - g3 * line_w[3]


def whiten_kernel(levels, area, rep_ref, *refs):
    x_refs, p_refs, q_refs = refs[:levels], refs[levels:2 * levels], refs[2 * levels:-1]
    out_ref = refs[-1]
    width = x_refs[0].shape[0]
    narrow = out_ref.shape[1]
    lane = lax.broadcasted_iota(jnp.int32, (8, width), 1)
    sub = lax.broadcasted_iota(jnp.int32, (8, width), 0)
    count = PANEL // 8
    lanes = lax.broadcasted_iota(jnp.int32, (width, width), 1)
    state, columns = [], []
    for m in range(levels):
        x, p = x_refs[m][...], p_refs[m]
        p = p[0] if len(p.shape) == 3 else p[...]
        q = q_refs[m - 1][...] if m else identity(width)
        pair = parts(x)
        state.append(q + product(pair, parts(p), ((1,), (1,))) * (1.0 / width))
        columns.append(pltpu.roll(x, width - rep_ref[0] * narrow, 1))
    done = [[] for _ in range(levels)]
    for top in range(0, width, PANEL):
        left = [[s[8 * j:8 * j + 8] for j in range(count)] for s in state]
        right = [[c[8 * j:8 * j + 8] for j in range(count)] if top == 0 else [] for c in columns]
        for kk in range(0, PANEL, 4):
            for m in range(levels):
                eliminate(left[m], right[m], top + kk, kk // 8, kk % 8, sub, area.at[m, kk // 4 % 2])
        for m in range(levels):
            for j in range(count):
                diagonal = jnp.sum(jnp.where(lane == sub + (top + 8 * j), left[m][j], 0.0), axis=1, keepdims=True)
                root = lax.rsqrt(diagonal)
                left[m][j] = left[m][j] * root
                if top == 0:
                    right[m][j] = right[m][j] * root
            upper = jnp.concatenate(left[m], axis=0)
            both = upper
            if top == 0:
                both = jnp.where(lanes[:PANEL] < narrow, jnp.concatenate(right[m], axis=0), upper)
            done[m].append(both)
            if top + PANEL < width:
                rest = state[m][PANEL:]
                if top == 0:
                    rest = jnp.where(lanes[PANEL:] < narrow, columns[m][PANEL:], rest)
                state[m] = rest - product(parts(upper.T[top + PANEL:]), parts(both))
    for m in range(levels):
        out_ref[m] = jnp.concatenate(done[m], axis=0).T[:narrow]


def last_kernel(levels, kind, side_ref, core_ref, rep_ref, own_ref, pair_ref, *refs):
    x_refs, p_refs, q_refs = refs[: levels - 1], refs[levels - 1:2 * levels - 1], refs[2 * levels - 1:-3]
    out_ref, x_last, area = refs[-3:]
    level_kernel(False, True, kind, False, side_ref, core_ref, own_ref, pair_ref, p_refs[-1], x_last)
    whiten_kernel(levels, area, rep_ref, *x_refs, x_last, *p_refs, *q_refs, out_ref)


def call(kernel, out_shape, n_smem, n_vmem, scratch=()):
    return pl.pallas_call(
        kernel,
        out_shape=out_shape,
        in_specs=[pl.BlockSpec(memory_space=pltpu.SMEM)] * n_smem
        + [pl.BlockSpec(memory_space=pltpu.VMEM)] * n_vmem,
        out_specs=jax.tree.map(lambda _: pl.BlockSpec(memory_space=pltpu.VMEM), out_shape),
        scratch_shapes=list(scratch),
        compiler_params=pltpu.CompilerParams(vmem_limit_bytes=VMEM_BYTES),
    )


def partner(leaf, bit):
    if bit == 0:
        return leaf ^ 1
    if bit == 1:
        return leaf ^ 2
    if bit == 2:
        return leaf ^ 6
    if bit == 4:
        return leaf ^ 24
    if bit == 5:
        return leaf ^ 56
    if bit == 6:
        return leaf ^ 120
    return leaf ^ (1 << bit)


def pair_gathered(value, axis, bit):
    leaves = range(lax.axis_size(axis))
    groups = [[leaf, partner(leaf, bit)] for leaf in leaves if not leaf >> bit & 1]
    return lax.all_gather(value, axis, axis=0, axis_index_groups=groups)


def swapped(value, axis, bit):
    pairs = [(source, partner(source, bit)) for source in range(lax.axis_size(axis))]
    return lax.ppermute(value, axis, pairs)


def local(basis, near_blocks, near_cols, bead_order):
    levels, narrow, rows = basis.shape
    block_rows, per_row = near_cols.shape
    blk = rows // block_rows
    reps = lax.axis_size("rep")
    width = reps * narrow
    leaf_index = lax.axis_index("leaf")
    rep_index = lax.axis_index("rep")
    rep_scalar = rep_index.astype(jnp.int32).reshape(1)
    square = jax.ShapeDtypeStruct((width, width), F32)

    def levels_of(rep):
        return lax.dynamic_slice_in_dim(basis, jnp.maximum(2 * rep - 1, 0), 2, 0)

    pieces = [levels_of(rep_index)]
    for shift in range(1, reps):
        pairs = [(source, (source + shift) % reps) for source in range(reps)]
        pieces.append(lax.ppermute(levels_of(lax.rem(rep_index + shift, reps)), "rep", pairs))
    tiles = near_blocks.reshape(block_rows * per_row, blk, blk)
    dense = [jax.ShapeDtypeStruct((rows, rows), BF16)] * 2
    high, low = call(dense_kernel, dense, 1, 2, [pltpu.VMEM((block_rows, rows, blk), F32)])(
        near_cols, tiles, bead_order
    )
    two = jax.ShapeDtypeStruct((2, width, width), F32)
    mine = call(panel_kernel, two, 1, reps + 2, [pltpu.VMEM((2, width, rows), F32)])(
        rep_scalar, *pieces, high, low
    )
    sent = lax.all_gather(mine, "rep", axis=0, tiled=True)
    core = (leaf_index & 1).astype(jnp.int32).reshape(1)
    half = panel = None
    x_list, p_list, q_list = [], [sent], []
    for bit in range(levels):
        first, last = bit == 0, bit == levels - 1
        kind = EXCHANGE[bit]
        value = half if kind[0] in "hp" and half is not None else sent[1:] if first else sent
        pair = (swapped if kind.endswith("other") else pair_gathered)(value, "leaf", bit)
        if kind.startswith("half"):
            pair = pair_gathered(pair, "leaf", 0)
        side = (leaf_index >> bit & 1).astype(jnp.int32).reshape(1)
        split = "" if last or EXCHANGE[bit + 1] in ("pair", "other") else EXCHANGE[bit + 1]
        shapes = [square]
        if not last:
            count = levels - bit - 1
            shapes += [square, square, jax.ShapeDtypeStruct((count, width, width), F32)]
            if split == "packed":
                shapes.append(jax.ShapeDtypeStruct((count * width - width // 4, width), F32))
            elif split:
                shapes.append(jax.ShapeDtypeStruct((count, width // 2, width), F32))
        kernel = functools.partial(level_kernel, first, last, kind, split)
        state = [] if first else [panel]
        if last:
            out = jax.ShapeDtypeStruct((levels, narrow, width), F32)
            kernel = functools.partial(last_kernel, levels, kind)
            scratch = [pltpu.VMEM((width, width), F32), pltpu.VMEM((levels, 2, 6, 8, width), F32)]
            return call(kernel, out, 3, 3 * levels, scratch)(
                side, core, rep_scalar, sent, pair, *x_list, *p_list, *q_list
            )
        x, panel, q, sent, *rest = call(kernel, shapes, 2, 2 + len(state))(side, core, sent, pair, *state)
        half = rest[0] if rest else None
        x_list.append(x)
        p_list.append(panel)
        q_list.append(q)


def solution(mesh):
    return jax.shard_map(
        local,
        mesh=mesh,
        in_specs=(P(None, "rep", "leaf"), P("leaf", None, None), P("leaf", None), P("leaf", None)),
        out_specs=P(None, "rep", "leaf"),
        check_vma=False,
    )
```
